32 devices in a mesh: rep: 8 (over y, x, core), exp: 4 (over z).
Axes of the slice: x: 2, y: 2, z: 4, core: 2. Of those that a mesh axis runs over, the one named last changes fastest.
Arguments:
- tubelets: bfloat16 [4096, 1536], P(('rep', 'exp')), may hold values from -6 to 6
- embed_weight: bfloat16 [1536, 1024], replicated, may hold values from -0.15625 to 0.15625
- norm_gain: float32 [1024], replicated, may hold values from 0.1 to 1.9
- routes: int32 [4096, 2], P(('rep', 'exp')), may hold values from 0 to 31, all different within a row; in each aligned block of 128 rows (0 to 127, 128 to 255, ...) at most 12 rows name the same one
- gate_codes: int32 [4096, 2], P(('rep', 'exp')), may hold values from 0 to 8
- w_in: bfloat16 [32, 1024, 4096], P('exp', None, 'rep'), may hold values from -0.1875 to 0.1875
- w_down: bfloat16 [32, 1024, 4096], P('exp', None, 'rep'), may hold values from -0.09375 to 0.09375
Outputs:
- layer_out: bfloat16 [4096, 1024], P(('rep', 'exp'))
The draws below stay inside these ranges and needn't reach their ends.
Inputs may be any that keep to these rules, and one draw needn't show every extreme that they name: Within each device's aligned block of 128 tokens no expert is named by more than 12 routes, a bound that some block reaches; a token's two experts differ.
All inputs are finite; a program needn't handle non-finite values.
Results may differ from the reference program's by a relative error of at most 0.012.
Values may be sent and summed in bfloat16 or wider, within the bound.
No kernel may reach another device: no remote copies, remote signals or barrier semaphores. Data moves between devices by JAX's collectives and lax.ppermute only.
A program may use at most 128 MiB of HBM per device.

```python
import math
import jax
import jax.numpy as jnp
import numpy as np
from jax import lax

D = 1024
FF = 4096
PATCH = 1536
TOK_DEV = 128
EXPERTS = 32
CAP = 12
TOKENS = 4096
N_REP = 8
N_EXP = 4


def set_ends(values, rng, least, high):
    extent = values.shape
    index_at = [jax.random.randint(jax.random.fold_in(rng, axis), (), 0, extent[axis]) for axis in range(len(extent))]
    values = values.at[tuple(index_at)].set(least)
    longest = extent.index(max(extent))
    index_at[longest] = (index_at[longest] + 1) % extent[longest]
    return values.at[tuple(index_at)].set(high)


def levels(stream_key, shape, cuts, low, high):
    loudness = 1.0
    for position, parts in cuts:
        heights = jax.random.uniform(jax.random.fold_in(jax.random.fold_in(stream_key, 6), position), (parts,), jnp.float32, low / len(cuts), high / len(cuts))
        loudness = loudness * jnp.repeat(jnp.exp(heights), shape[position] // parts).reshape((-1,) + (1,) * (len(shape) - 1 - position))
    return loudness


def deal_out(key, own, number, rows, number_of, top, bound, lean):
    ranking = jax.random.permutation(key, number_of)
    heavy_load, usual = portions_of(number_of, rows * top, bound, lean, True), portions_of(number_of, rows * top, bound, lean, False)
    places = jnp.arange(number_of)

    def named(sizes, rotation):
        used = int((sizes > 0).sum())
        fixed = max(1, used // 4)
        moved = fixed + (places - fixed + rotation * (used - fixed)) % max(1, number_of - fixed)
        return jnp.zeros((number_of,), jnp.int32).at[ranking[jnp.where(places < fixed, places, moved)]].set(jnp.asarray(sizes, jnp.int32))

    sizes = jnp.where(number % 4 == 0, named(heavy_load, number // 4), named(usual, number - number // 4 - 1))
    mixed = jax.random.permutation(jax.random.fold_in(own, 3), number_of)
    giver, sink = mixed[0:number_of // 2 * 2:2], mixed[1:number_of // 2 * 2:2]
    room = jnp.minimum(sizes[giver] - 1, bound - sizes[sink]) // 2
    room = jnp.where((giver == ranking[0]) | (sink == ranking[0]) | (sizes[sink] == 0), 0, jnp.maximum(room, 0))
    moved = jax.random.randint(jax.random.fold_in(own, 4), (number_of // 2,), 0, 1 << 20) % (room + 1)
    sizes = sizes.at[giver].add(-moved).at[sink].add(moved)
    members = jnp.searchsorted(jnp.cumsum(sizes), jnp.arange(rows * top), side="right").astype(jnp.int32)
    listing = members.reshape(top, rows).T
    listing = listing[jax.random.permutation(jax.random.fold_in(own, 1), rows)]
    rotation = jax.random.randint(jax.random.fold_in(own, 2), (rows, 1), 0, top)
    return jnp.take_along_axis(listing, (jnp.arange(top)[None, :] + rotation) % top, axis=1)


def portions_of(amount, total, reach, slope, full):
    weights = [(1 << 20) // math.isqrt(grade ** slope) + 1 for grade in range(1, amount + 1)]
    largest = reach if full else min(reach, max(-(-total // amount), total * weights[0] // sum(weights)))
    least = 1 if total - largest >= amount - 1 else 0
    given, spare = [largest] + [least] * (amount - 1), total - largest - least * (amount - 1)
    while spare > 0:
        movable = [i for i in range(1, amount) if given[i] < largest] or [i for i in range(1, amount) if given[i] < reach]
        whole, budget = sum([weights[i] for i in movable]), spare
        for i in movable:
            extra = min(reach - given[i], max(1, budget * weights[i] // whole), spare)
            given[i] = given[i] + extra
            spare = spare - extra
    return np.array(given)


def noise(key, shape, spread, most, cuts=(), kind=jnp.bfloat16):
    array = jax.random.normal(key, shape, jnp.float32) * spread
    if len(cuts) > 0:
        array = levels(key, shape, cuts, -0.22, 0.18) * array
    return jnp.clip(array, min=-most, max=most).astype(kind)


def setup_inputs(seed: int = 0) -> dict:
    splits = jax.random.split(jax.random.key(seed), 8)
    tubelets = noise(splits[0], (TOKENS, PATCH), 1.0, 6.0, ((0, 32),))
    embed_weight = noise(splits[1], (PATCH, D), PATCH ** -0.5, 0.15625)
    norm_gain = jnp.clip(1.0 + 0.18 * jax.random.normal(splits[2], (D,), jnp.float32), 0.1, 1.9)
    routes_keys = jax.random.split(jax.random.fold_in(splits[3], 1), TOKENS // TOK_DEV)
    routes_turns = jax.random.permutation(jax.random.fold_in(splits[3], 3), TOKENS // TOK_DEV)
    routes = jax.vmap(lambda own, number: deal_out(jax.random.fold_in(splits[3], 2), own, number, TOK_DEV, EXPERTS, 2, CAP, 2))(routes_keys, routes_turns).reshape((TOKENS, 2))
    gate_codes = set_ends(jax.random.randint(splits[4], (TOKENS, 2), 0, 9), jax.random.fold_in(splits[4], 1), 0, 8).astype(jnp.int32)
    w_in = noise(splits[5], (EXPERTS, D, FF), D ** -0.5, 0.1875, ((0, 4), (2, 8)))
    w_down = noise(splits[6], (EXPERTS, D, FF), FF ** -0.5, 0.09375, ((0, 4), (2, 8)))
    return {"tubelets": tubelets, "embed_weight": embed_weight, "norm_gain": norm_gain, "routes": routes, "gate_codes": gate_codes, "w_in": w_in, "w_down": w_down}


def layer_norm(values, norm_gain):
    floats = values.astype(jnp.float32)
    average = lax.optimization_barrier(jnp.mean(floats, axis=-1, keepdims=True))
    centred = floats - average
    variance = lax.optimization_barrier(jnp.mean(centred * centred, axis=-1, keepdims=True))
    return (centred * lax.rsqrt(variance + 1e-06) * norm_gain).astype(jnp.bfloat16)

def expert_apply(packed):
    expert_rows, panel_in, panel_down = packed
    hidden = jax.nn.gelu(jnp.dot(expert_rows.astype(jnp.float32), panel_in.astype(jnp.float32), preferred_element_type=jnp.float32)).astype(jnp.bfloat16)
    return jnp.dot(hidden.astype(jnp.float32), panel_down.astype(jnp.float32).T, preferred_element_type=jnp.float32).astype(jnp.bfloat16)

def reference(tubelets, embed_weight, norm_gain, routes, gate_codes, w_in, w_down):
    embedded = jnp.dot(tubelets, embed_weight, preferred_element_type=jnp.float32).astype(jnp.bfloat16)
    normed = layer_norm(embedded, norm_gain)
    blocks = N_REP * N_EXP
    block_routes = routes.reshape(blocks, 2 * TOK_DEV)
    onehot = (block_routes[:, :, None] == jnp.arange(EXPERTS, dtype=jnp.int32)[None, None, :]).astype(jnp.int32)
    slot_rank = lax.optimization_barrier(jnp.sum((jnp.cumsum(onehot, axis=1) - 1) * onehot, axis=2)).astype(jnp.int32)
    block_ids = jnp.arange(blocks, dtype=jnp.int32)[:, None] * jnp.ones((1, 2 * TOK_DEV), jnp.int32)
    target = (block_routes * (blocks * CAP) + block_ids * CAP + slot_rank).reshape(-1).astype(jnp.int32)
    rows_rep = jnp.repeat(normed, 2, axis=0)
    buffer = jnp.zeros((EXPERTS * blocks * CAP, D), jnp.bfloat16).at[target].set(rows_rep)
    buffer = buffer.reshape(EXPERTS, blocks * CAP, D)
    outputs = lax.map(expert_apply, (buffer, w_in, w_down))
    picked = outputs.reshape(-1, D)[target].astype(jnp.float32)
    gate_vals = 0.25 + 0.125 * gate_codes.reshape(-1).astype(jnp.float32)
    combined = lax.optimization_barrier(jnp.sum((picked * gate_vals[:, None]).reshape(TOKENS, 2, D), axis=1))
    return (embedded.astype(jnp.float32) + combined).astype(jnp.bfloat16)
```

```python
import functools

import jax
import jax.numpy as jnp
from jax import lax
from jax.experimental import pallas as pl
from jax.experimental.pallas import tpu as pltpu
from jax.sharding import PartitionSpec as P

F32 = jnp.float32
BF16 = jnp.bfloat16
CHUNKS = 2
CORE, NEAR_A, NEAR_B = 0, 1, 2
GROUP_BITS = 3
VMEM_LIMIT = 50 * 1024 * 1024


def swapped(array, axis, distance):
    return lax.ppermute(array, axis, [(i, i ^ distance) for i in range(lax.axis_size(axis))])


def mm(a, b, dims=((1,), (0,))):
    return lax.dot_general(a, b, (dims, ((), ())), preferred_element_type=F32)


def vmem():
    return pl.BlockSpec(memory_space=pltpu.VMEM)


def smem():
    return pl.BlockSpec(memory_space=pltpu.SMEM)


def dispatch_kernel(n_exp, half, cap, place_ref, own_ref, sib_ref, weight_ref, gain_ref, code_ref, sib_code_ref,
                    emb_ref, gate_ref, *piece_refs):
    tok = own_ref.shape[0]
    both = 2 * tok
    count = n_exp * half
    slots = 2 * cap
    rows = count * slots
    gain = gain_ref[...]

    def normed_of(ref, keep):
        embedded = mm(ref[...], weight_ref[...]).astype(BF16)
        if keep:
            emb_ref[...] = embedded
        floats = embedded.astype(F32)
        centred = floats - jnp.mean(floats, axis=-1, keepdims=True)
        variance = jnp.mean(centred * centred, axis=-1, keepdims=True)
        return (centred * lax.rsqrt(variance + 1e-06) * gain).astype(BF16)

    normed = jnp.concatenate([normed_of(own_ref, True), normed_of(sib_ref, False)], axis=0)
    codes = jnp.concatenate([code_ref[...], sib_code_ref[...]], axis=0)
    plane, core = place_ref[0], place_ref[1]

    column = lax.broadcasted_iota(jnp.int32, (both, count), 1)
    expert = (plane ^ (column // half)) * (2 * half) + core * half + column % half
    first = codes[:, 0:1] == expert
    second = codes[:, 1:2] == expert
    member = jnp.where(first | second, 1.0, 0.0)
    gates = 0.25 + 0.125 * codes[:, 2:4].astype(F32)
    gated = jnp.where(first, gates[:, 0:1], 0.0) + jnp.where(second, gates[:, 1:2], 0.0)
    earlier_t = lax.broadcasted_iota(jnp.int32, (both, both), 0)
    later_t = lax.broadcasted_iota(jnp.int32, (both, both), 1)
    same = (earlier_t // tok) == (later_t // tok)
    before = jnp.where(same & (earlier_t < later_t), 1.0, 0.0).astype(BF16)
    after = jnp.where(same & (later_t < earlier_t), 1.0, 0.0).astype(BF16)
    equal = jnp.where(earlier_t == later_t, 1.0, 0.0).astype(BF16)
    member16 = member.astype(BF16)
    rank_t = mm(member16, before, ((0,), (0,)))
    member_t = mm(member16, equal, ((0,), (0,)))
    block_t = jnp.where(lax.broadcasted_iota(jnp.int32, (count, both), 1) >= tok, float(cap), 0.0)
    pos_t = jnp.where(member_t > 0.5, rank_t + block_t, -1.0).astype(BF16)
    spread = jnp.where(
        lax.broadcasted_iota(jnp.int32, (rows, count), 0) // slots
        == lax.broadcasted_iota(jnp.int32, (rows, count), 1), 1.0, 0.0).astype(BF16)
    slot_t = (lax.broadcasted_iota(jnp.int32, (rows, both), 0) % slots).astype(F32)
    select = jnp.where(mm(spread, pos_t) == slot_t, 1.0, 0.0).astype(BF16)
    buffer = mm(select, normed)
    for index, ref in enumerate(piece_refs):
        per = ref.shape[0]
        for e in range(per):
            start = (index * per + e) * slots
            ref[e] = buffer[start:start + slots].astype(BF16)

    rank = mm(after, member16)
    block = jnp.where(lax.broadcasted_iota(jnp.int32, (both, count), 0) >= tok, float(cap), 0.0)
    pos = jnp.where(member > 0.5, rank + block, -1.0).astype(BF16)
    slot = (lax.broadcasted_iota(jnp.int32, (both, rows), 1) % slots).astype(F32)
    spread_gate = mm(gated.astype(BF16), spread, ((1,), (1,)))
    gate_ref[...] = jnp.where(mm(pos, spread, ((1,), (1,))) == slot, spread_gate, 0.0).astype(BF16)


def dispatch(place, own, sib, weight, gain, codes, sib_codes, n_exp, half, cap):
    tok, width = own.shape[0], weight.shape[1]
    rows = n_exp * half * 2 * cap
    per = half // CHUNKS
    outs = [jax.ShapeDtypeStruct((tok, width), BF16), jax.ShapeDtypeStruct((2 * tok, rows), BF16)]
    outs += [jax.ShapeDtypeStruct((per, 2 * cap, width), BF16)] * (n_exp * CHUNKS)
    result = pl.pallas_call(
        functools.partial(dispatch_kernel, n_exp, half, cap),
        out_shape=outs,
        in_specs=[smem()] + [vmem()] * 6,
        out_specs=[vmem()] * len(outs),
        compiler_params=pltpu.CompilerParams(vmem_limit_bytes=VMEM_LIMIT),
        cost_estimate=pl.CostEstimate(
            flops=4 * tok * own.shape[1] * width, bytes_accessed=weight.size * 2 + rows * width * 2, transcendentals=0),
        name="dispatch",
    )(place, own, sib, weight, gain.reshape(1, width), codes, sib_codes)
    pieces = result[2:]
    return result[0], result[1], [[pieces[s * CHUNKS + c] for s in range(n_exp)] for c in range(CHUNKS)]


def experts_kernel(place_ref, own_ref, a_ref, b_ref, d1_ref, d2_ref, in_own_ref, in_sib_ref, down_own_ref, down_sib_ref,
                   p_own_ref, p_a_ref, p_b_ref, p_d1_ref, p_d2_ref, x_ref, acc_ref):
    e, f = pl.program_id(0), pl.program_id(1)
    split = pl.num_programs(0) // 2
    m = own_ref.shape[1]

    @pl.when(f == 0)
    def _():
        x_ref[0:m] = own_ref[0]
        x_ref[m:2 * m] = a_ref[0]
        x_ref[2 * m:3 * m] = b_ref[0]

        @pl.when(e < split)
        def _():
            x_ref[3 * m:4 * m] = d1_ref[0]

        @pl.when(e >= split)
        def _():
            x_ref[3 * m:4 * m] = d2_ref[0]

    x = x_ref[...]
    h_own = jax.nn.gelu(mm(x, in_own_ref[0])).astype(BF16)
    h_sib = jax.nn.gelu(mm(x, in_sib_ref[0])).astype(BF16)
    total = mm(h_own, down_own_ref[0], ((1,), (1,))) + mm(h_sib, down_sib_ref[0], ((1,), (1,)))

    @pl.when(f == 0)
    def _():
        acc_ref[...] = total

    @pl.when(f > 0)
    def _():
        acc_ref[...] += total

    @pl.when(f == pl.num_programs(1) - 1)
    def _():
        p_own_ref[0] = acc_ref[0:m].astype(BF16)
        p_a_ref[0] = acc_ref[m:2 * m].astype(BF16)
        p_b_ref[0] = acc_ref[2 * m:3 * m].astype(BF16)

        @pl.when(e < split)
        def _():
            p_d1_ref[0] = acc_ref[3 * m:4 * m].astype(BF16)

        @pl.when(e >= split)
        def _():
            p_d2_ref[0] = acc_ref[3 * m:4 * m].astype(BF16)


def experts(place, chunk, own, near_a, near_b, d1, d2, in_own, in_sib, down_own, down_sib):
    per, m, width = own.shape
    half = in_sib.shape[0]
    ff = in_sib.shape[2]
    steps = 2 if ff % 512 == 0 else 1
    fb = ff // steps
    split = per // 2
    rows = pl.BlockSpec((1, m, width), lambda e, f, p: (e, 0, 0))
    rows1 = pl.BlockSpec((1, m, width), lambda e, f, p: (jnp.minimum(e, split - 1), 0, 0))
    rows2 = pl.BlockSpec((1, m, width), lambda e, f, p: (jnp.maximum(e - split, 0), 0, 0))
    w_own = pl.BlockSpec((1, width, fb), lambda e, f, p: (p[1] * half + chunk * per + e, 0, f))
    w_sib = pl.BlockSpec((1, width, fb), lambda e, f, p: (chunk * per + e, 0, f))
    shape = jax.ShapeDtypeStruct(own.shape, BF16)
    part = jax.ShapeDtypeStruct(d1.shape, BF16)
    return pl.pallas_call(
        experts_kernel,
        out_shape=[shape, shape, shape, part, part],
        grid_spec=pltpu.PrefetchScalarGridSpec(
            num_scalar_prefetch=1,
            grid=(per, steps),
            in_specs=[rows, rows, rows, rows1, rows2, w_own, w_sib, w_own, w_sib],
            out_specs=[rows, rows, rows, rows1, rows2],
            scratch_shapes=[pltpu.VMEM((4 * m, width), BF16), pltpu.VMEM((4 * m, width), F32)],
        ),
        compiler_params=pltpu.CompilerParams(
            vmem_limit_bytes=VMEM_LIMIT, dimension_semantics=("arbitrary", "arbitrary")),
        cost_estimate=pl.CostEstimate(
            flops=2 * per * 4 * m * width * 2 * ff * 2, bytes_accessed=per * width * ff * 8 + per * m * width * 16,
            transcendentals=per * 4 * m * 2 * ff),
        name="experts",
    )(place, own, near_a, near_b, d1, d2, in_own, in_sib, down_own, down_sib)


def combine_kernel(tok, gate_ref, emb_ref, *refs):
    piece_refs, (mine_ref, send_ref, rows_ref) = refs[:-3], refs[-3:]
    per, slots, _ = piece_refs[0].shape
    for index, ref in enumerate(piece_refs):
        for e in range(per):
            start = (index * per + e) * slots
            rows_ref[start:start + slots] = ref[e].astype(F32)
    total = mm(gate_ref[...], rows_ref[...].astype(BF16))
    mine_ref[...] = total[0:tok] + emb_ref[...].astype(F32)
    send_ref[...] = total[tok:2 * tok].astype(BF16)


def combine(gate, embedded, pieces):
    tok, width = embedded.shape
    rows = gate.shape[1]
    return pl.pallas_call(
        functools.partial(combine_kernel, tok),
        out_shape=[jax.ShapeDtypeStruct((tok, width), F32), jax.ShapeDtypeStruct((tok, width), BF16)],
        in_specs=[vmem()] * (2 + len(pieces)),
        out_specs=[vmem()] * 2,
        scratch_shapes=[pltpu.VMEM((rows, width), F32)],
        compiler_params=pltpu.CompilerParams(vmem_limit_bytes=VMEM_LIMIT),
        cost_estimate=pl.CostEstimate(flops=4 * tok * rows * width, bytes_accessed=rows * width * 2, transcendentals=0),
        name="combine",
    )(gate, embedded, *pieces)


def on_device(tubelets, embed_weight, norm_gain, routes, gate_codes, w_in, w_down):
    tok = tubelets.shape[0]
    n_exp = lax.axis_size("exp")
    half = w_in.shape[0] // 2
    cap = 3 * tok // (w_in.shape[0] * n_exp)
    position = lax.axis_index("rep")
    core = position % 2
    place = jnp.stack([lax.axis_index("exp"), core]).astype(jnp.int32)

    codes = jnp.concatenate([routes, gate_codes], axis=1)
    sib_codes = swapped(codes, "rep", 1 << CORE)
    sib_tubelets = swapped(tubelets, "rep", 1 << CORE)

    for bit in range(GROUP_BITS, lax.axis_size("rep").bit_length() - 1):
        upper = position // (1 << bit) % 2 == 1

        def gathered(panel):
            partner = swapped(panel, "rep", 1 << bit)
            return jnp.where(upper, jnp.concatenate([partner, panel], axis=2), jnp.concatenate([panel, partner], axis=2))

        w_in, w_down = gathered(w_in), gathered(w_down)

    embedded, gate, pieces = dispatch(
        place, tubelets, sib_tubelets, embed_weight, norm_gain, codes, sib_codes, n_exp, half, cap)

    in_sib = swapped(lax.dynamic_slice_in_dim(w_in, (1 - core) * half, half, 0), "rep", 1 << CORE)
    down_sib = swapped(lax.dynamic_slice_in_dim(w_down, (1 - core) * half, half, 0), "rep", 1 << CORE)

    returned = []
    for chunk in range(CHUNKS):
        arrived = [pieces[chunk][0]] + [swapped(pieces[chunk][s], "exp", s) for s in range(1, n_exp)]
        own = jnp.concatenate(arrived, axis=1)
        split = own.shape[0] // 2
        near_a = swapped(own, "rep", 1 << NEAR_A)
        near_b = swapped(own, "rep", 1 << NEAR_B)
        d1 = swapped(near_a[:split], "rep", 1 << NEAR_B)
        d2 = swapped(near_b[split:], "rep", 1 << NEAR_A)
        p_own, p_a, p_b, p_d1, p_d2 = experts(
            place, chunk, own, near_a, near_b, d1, d2, w_in, in_sib, w_down, down_sib)
        r1 = swapped(p_d1, "rep", 1 << NEAR_A)
        r2 = swapped(p_d2, "rep", 1 << NEAR_B)
        to_b = jnp.concatenate([p_b[:split] + r1, p_b[split:]], axis=0)
        to_a = jnp.concatenate([p_a[:split], p_a[split:] + r2], axis=0)
        from_a = swapped(to_a, "rep", 1 << NEAR_A)
        from_b = swapped(to_b, "rep", 1 << NEAR_B)
        done = (p_own.astype(F32) + from_a.astype(F32) + from_b.astype(F32)).astype(BF16)
        done = done.reshape(done.shape[0], n_exp, 2 * cap, done.shape[2])
        returned.append([done[:, 0]] + [swapped(done[:, s], "exp", s) for s in range(1, n_exp)])

    pieces_back = [returned[c][s] for s in range(n_exp) for c in range(CHUNKS)]
    mine, send = combine(gate, embedded, pieces_back)
    other = swapped(send, "rep", 1 << CORE)
    return (mine + other.astype(F32)).astype(BF16)


def solution(mesh):
    return jax.shard_map(
        on_device,
        mesh=mesh,
        in_specs=(
            P(("rep", "exp"), None),
            P(),
            P(),
            P(("rep", "exp"), None),
            P(("rep", "exp"), None),
            P("exp", None, "rep"),
            P("exp", None, "rep"),
        ),
        out_specs=P(("rep", "exp"), None),
        check_vma=False,
    )
```

```python
import functools

import jax
import jax.numpy as jnp
from jax import lax
from jax.experimental import pallas as pl
from jax.experimental.pallas import tpu as pltpu
from jax.sharding import PartitionSpec as P

F32 = jnp.float32
BF16 = jnp.bfloat16
CHUNKS = 2
CORE, NEAR_A, NEAR_B = 0, 1, 2
GROUP_BITS = 3
VMEM_LIMIT = 16 * 1024 * 1024


def swapped(array, axis, distance):
    return lax.ppermute(array, axis, [(i, i ^ distance) for i in range(lax.axis_size(axis))])


def after(value, *others):
    return lax.optimization_barrier((value, *others))[0]


def mm(a, b, dims=((1,), (0,))):
    return lax.dot_general(a, b, (dims, ((), ())), preferred_element_type=F32)


def vmem():
    return pl.BlockSpec(memory_space=pltpu.VMEM)


def smem():
    return pl.BlockSpec(memory_space=pltpu.SMEM)


def embed_kernel(tubelets_ref, weight_ref, gain_ref, emb_ref, normed_ref):
    embedded = mm(tubelets_ref[...], weight_ref[...]).astype(BF16)
    emb_ref[...] = embedded
    floats = embedded.astype(F32)
    centred = floats - jnp.mean(floats, axis=-1, keepdims=True)
    variance = jnp.mean(centred * centred, axis=-1, keepdims=True)
    normed_ref[...] = (centred * lax.rsqrt(variance + 1e-06) * gain_ref[...]).astype(BF16)


def embed(tubelets, weight, gain):
    tok, width = tubelets.shape[0], weight.shape[1]
    shape = jax.ShapeDtypeStruct((tok, width), BF16)
    return pl.pallas_call(
        embed_kernel,
        out_shape=[shape, shape],
        in_specs=[vmem()] * 3,
        out_specs=[vmem()] * 2,
        compiler_params=pltpu.CompilerParams(vmem_limit_bytes=VMEM_LIMIT),
        cost_estimate=pl.CostEstimate(flops=2 * tok * weight.size, bytes_accessed=weight.size * 2, transcendentals=0),
        name="embed",
    )(tubelets, weight, gain.reshape(1, width))


def route_kernel(n_exp, half, cap, place_ref, route_ref, sib_route_ref, code_ref, sib_code_ref, select_ref, gate_ref):
    tok = route_ref.shape[0]
    both = 2 * tok
    count = n_exp * half
    slots = 2 * cap
    rows = count * slots
    routes = jnp.concatenate([route_ref[...], sib_route_ref[...]], axis=0)
    codes = jnp.concatenate([code_ref[...], sib_code_ref[...]], axis=0)
    plane, core = place_ref[0], place_ref[1]

    column = lax.broadcasted_iota(jnp.int32, (both, count), 1)
    expert = (plane ^ (column // half)) * (2 * half) + core * half + column % half
    first = routes[:, 0:1] == expert
    second = routes[:, 1:2] == expert
    member = jnp.where(first | second, 1.0, 0.0)
    gates = 0.25 + 0.125 * codes.astype(F32)
    gated = jnp.where(first, gates[:, 0:1], 0.0) + jnp.where(second, gates[:, 1:2], 0.0)
    earlier_t = lax.broadcasted_iota(jnp.int32, (both, both), 0)
    later_t = lax.broadcasted_iota(jnp.int32, (both, both), 1)
    same = (earlier_t // tok) == (later_t // tok)
    before = jnp.where(same & (earlier_t < later_t), 1.0, 0.0).astype(BF16)
    after_t = jnp.where(same & (later_t < earlier_t), 1.0, 0.0).astype(BF16)
    equal = jnp.where(earlier_t == later_t, 1.0, 0.0).astype(BF16)
    member16 = member.astype(BF16)
    rank_t = mm(member16, before, ((0,), (0,)))
    member_t = mm(member16, equal, ((0,), (0,)))
    block_t = jnp.where(lax.broadcasted_iota(jnp.int32, (count, both), 1) >= tok, float(cap), 0.0)
    pos_t = jnp.where(member_t > 0.5, rank_t + block_t, -1.0).astype(BF16)
    spread = jnp.where(
        lax.broadcasted_iota(jnp.int32, (rows, count), 0) // slots
        == lax.broadcasted_iota(jnp.int32, (rows, count), 1), 1.0, 0.0).astype(BF16)
    slot_t = (lax.broadcasted_iota(jnp.int32, (rows, both), 0) % slots).astype(F32)
    select_ref[...] = jnp.where(mm(spread, pos_t) == slot_t, 1.0, 0.0).astype(BF16)

    rank = mm(after_t, member16)
    block = jnp.where(lax.broadcasted_iota(jnp.int32, (both, count), 0) >= tok, float(cap), 0.0)
    pos = jnp.where(member > 0.5, rank + block, -1.0).astype(BF16)
    slot = (lax.broadcasted_iota(jnp.int32, (both, rows), 1) % slots).astype(F32)
    spread_gate = mm(gated.astype(BF16), spread, ((1,), (1,)))
    gate_ref[...] = jnp.where(mm(pos, spread, ((1,), (1,))) == slot, spread_gate, 0.0).astype(BF16)


def route(place, routes, sib_routes, codes, sib_codes, n_exp, half, cap):
    both = 2 * routes.shape[0]
    rows = n_exp * half * 2 * cap
    return pl.pallas_call(
        functools.partial(route_kernel, n_exp, half, cap),
        out_shape=[jax.ShapeDtypeStruct((rows, both), BF16), jax.ShapeDtypeStruct((both, rows), BF16)],
        in_specs=[smem()] + [vmem()] * 4,
        out_specs=[vmem()] * 2,
        compiler_params=pltpu.CompilerParams(vmem_limit_bytes=VMEM_LIMIT),
        cost_estimate=pl.CostEstimate(flops=2 * rows * both * 64, bytes_accessed=rows * both * 4, transcendentals=0),
        name="route",
    )(place, routes, sib_routes, codes, sib_codes)


def pack_kernel(select_ref, normed_ref, sib_ref, *piece_refs):
    buffer = mm(select_ref[...], jnp.concatenate([normed_ref[...], sib_ref[...]], axis=0))
    per, slots, _ = piece_refs[0].shape
    for index, ref in enumerate(piece_refs):
        for e in range(per):
            start = (index * per + e) * slots
            ref[e] = buffer[start:start + slots].astype(BF16)


def pack(select, normed, sib_normed, n_exp, half, cap):
    width = normed.shape[1]
    rows = select.shape[0]
    shape = jax.ShapeDtypeStruct((half // CHUNKS, 2 * cap, width), BF16)
    pieces = pl.pallas_call(
        pack_kernel,
        out_shape=[shape] * (n_exp * CHUNKS),
        in_specs=[vmem()] * 3,
        out_specs=[vmem()] * (n_exp * CHUNKS),
        compiler_params=pltpu.CompilerParams(vmem_limit_bytes=VMEM_LIMIT),
        cost_estimate=pl.CostEstimate(
            flops=2 * select.size * width, bytes_accessed=rows * width * 4, transcendentals=0),
        name="pack",
    )(select, normed, sib_normed)
    return [[pieces[s * CHUNKS + c] for s in range(n_exp)] for c in range(CHUNKS)]


def experts_kernel(chunk, half, place_ref, own_ref, a_ref, b_ref, d1_ref, d2_ref,
                   in_own_ref, in_sib_ref, down_own_ref, down_sib_ref,
                   p_own_ref, p_a_ref, p_b_ref, p_d1_ref, p_d2_ref, h_ref):
    per, m, _ = own_ref.shape
    split = per // 2
    ff = in_own_ref.shape[2]
    for e in range(per):
        index = place_ref[1] * half + chunk * per + e
        diagonal, p_diagonal = (d1_ref, p_d1_ref) if e < split else (d2_ref, p_d2_ref)
        x = jnp.concatenate([own_ref[e], a_ref[e], b_ref[e], diagonal[e % split]], axis=0)
        h_ref[:, 0:ff] = jax.nn.gelu(mm(x, in_own_ref[index])).astype(BF16)
        h_ref[:, ff:] = jax.nn.gelu(mm(x, in_sib_ref[index])).astype(BF16)
        total = mm(h_ref[:, 0:ff], down_own_ref[index], ((1,), (1,))) + mm(
            h_ref[:, ff:], down_sib_ref[index], ((1,), (1,)))
        p_own_ref[e] = total[0:m].astype(BF16)
        p_a_ref[e] = total[m:2 * m].astype(BF16)
        p_b_ref[e] = total[2 * m:3 * m].astype(BF16)
        p_diagonal[e % split] = total[3 * m:4 * m].astype(BF16)


def experts(place, chunk, own, near_a, near_b, d1, d2, in_own, in_sib, down_own, down_sib):
    per, m, width = own.shape
    count, _, ff = in_own.shape
    shape = jax.ShapeDtypeStruct(own.shape, BF16)
    part = jax.ShapeDtypeStruct(d1.shape, BF16)
    return pl.pallas_call(
        functools.partial(experts_kernel, chunk, count // 2),
        out_shape=[shape, shape, shape, part, part],
        in_specs=[smem()] + [vmem()] * 9,
        out_specs=[vmem()] * 5,
        scratch_shapes=[pltpu.VMEM((4 * m, 2 * ff), BF16)],
        compiler_params=pltpu.CompilerParams(vmem_limit_bytes=VMEM_LIMIT),
        cost_estimate=pl.CostEstimate(
            flops=2 * per * 4 * m * width * 2 * ff * 2, bytes_accessed=per * m * width * 16,
            transcendentals=per * 4 * m * 2 * ff),
        name="experts",
    )(place, own, near_a, near_b, d1, d2, in_own, in_sib, down_own, down_sib)


def combine_kernel(tok, gate_ref, emb_ref, *refs):
    piece_refs, (mine_ref, send_ref, rows_ref) = refs[:-3], refs[-3:]
    per, slots, _ = piece_refs[0].shape
    for index, ref in enumerate(piece_refs):
        for e in range(per):
            start = (index * per + e) * slots
            rows_ref[start:start + slots] = ref[e].astype(F32)
    total = mm(gate_ref[...], rows_ref[...].astype(BF16))
    mine_ref[...] = total[0:tok] + emb_ref[...].astype(F32)
    send_ref[...] = total[tok:2 * tok].astype(BF16)


def combine(gate, embedded, pieces):
    tok, width = embedded.shape
    rows = gate.shape[1]
    return pl.pallas_call(
        functools.partial(combine_kernel, tok),
        out_shape=[jax.ShapeDtypeStruct((tok, width), F32), jax.ShapeDtypeStruct((tok, width), BF16)],
        in_specs=[vmem()] * (2 + len(pieces)),
        out_specs=[vmem()] * 2,
        scratch_shapes=[pltpu.VMEM((rows, width), F32)],
        compiler_params=pltpu.CompilerParams(vmem_limit_bytes=VMEM_LIMIT),
        cost_estimate=pl.CostEstimate(flops=4 * tok * rows * width, bytes_accessed=rows * width * 2, transcendentals=0),
        name="combine",
    )(gate, embedded, *pieces)


def on_device(tubelets, embed_weight, norm_gain, routes, gate_codes, w_in, w_down):
    tok = tubelets.shape[0]
    n_exp = lax.axis_size("exp")
    half = w_in.shape[0] // 2
    cap = 3 * tok // (w_in.shape[0] * n_exp)
    position = lax.axis_index("rep")
    core = position % 2
    place = jnp.stack([lax.axis_index("exp"), core]).astype(jnp.int32)

    core_bit = 1 << CORE
    sib_routes = swapped(routes, "rep", core_bit)
    sib_codes = swapped(gate_codes, "rep", core_bit)
    embedded, normed = embed(tubelets, embed_weight, norm_gain)
    sib_normed = swapped(normed, "rep", core_bit)
    select, gate = route(place, routes, sib_routes, gate_codes, sib_codes, n_exp, half, cap)

    for bit in range(GROUP_BITS, lax.axis_size("rep").bit_length() - 1):
        upper = position // (1 << bit) % 2 == 1

        def gathered(panel):
            partner = swapped(panel, "rep", 1 << bit)
            return jnp.where(upper, jnp.concatenate([partner, panel], axis=2), jnp.concatenate([panel, partner], axis=2))

        w_in, w_down = gathered(w_in), gathered(w_down)

    in_sib = swapped(after(w_in, sib_normed, select), "rep", core_bit)
    down_sib = swapped(after(w_down, sib_normed, select), "rep", core_bit)
    pieces = pack(select, normed, sib_normed, n_exp, half, cap)

    def from_planes(leaving):
        arrived = [leaving[0]] + [swapped(leaving[s], "exp", s) for s in range(1, n_exp)]
        return jnp.concatenate(arrived, axis=1)

    def to_planes(p_own, from_a, from_b):
        done = (p_own.astype(F32) + from_a.astype(F32) + from_b.astype(F32)).astype(BF16)
        done = done.reshape(done.shape[0], n_exp, 2 * cap, done.shape[2])
        return [done[:, 0]] + [swapped(done[:, s], "exp", s) for s in range(1, n_exp)]

    split = half // CHUNKS // 2
    a_bit, b_bit = 1 << NEAR_A, 1 << NEAR_B

    def reduced(parts, r):
        _, p_a, p_b, _, _ = parts
        to_b = jnp.concatenate([p_b[:split] + r[0], p_b[split:]], axis=0)
        to_a = jnp.concatenate([p_a[:split], p_a[split:] + r[1]], axis=0)
        return to_a, to_b

    early1 = swapped(pieces[1][1], "exp", 1)
    own0 = from_planes(pieces[0])
    late1 = lax.optimization_barrier((*pieces[1][2:], own0, in_sib))[:n_exp - 2]
    own1 = jnp.concatenate(
        [pieces[1][0], early1] + [swapped(piece, "exp", s + 2) for s, piece in enumerate(late1)], axis=1)
    a0, b0 = swapped(own0, "rep", a_bit), swapped(own0, "rep", b_bit)
    own1 = after(own1, a0, b0)
    d0 = swapped(a0[:split], "rep", b_bit), swapped(b0[split:], "rep", a_bit)
    a1, b1 = swapped(own1, "rep", a_bit), swapped(own1, "rep", b_bit)
    parts0 = experts(place, 0, own0, a0, b0, *d0, w_in, in_sib, w_down, down_sib)
    a1, b1, *parts0 = lax.optimization_barrier((a1, b1, *parts0))
    d1 = swapped(a1[:split], "rep", b_bit), swapped(b1[split:], "rep", a_bit)
    r0 = swapped(parts0[3], "rep", a_bit), swapped(parts0[4], "rep", b_bit)
    to_a0, to_b0 = reduced(parts0, r0)
    to_a0, to_b0, *d1 = lax.optimization_barrier((to_a0, to_b0, *d1))
    from_a0, from_b0 = swapped(to_a0, "rep", a_bit), swapped(to_b0, "rep", b_bit)
    parts1 = experts(place, 1, own1, a1, b1, *d1, w_in, in_sib, w_down, down_sib)
    *parts1, from_a0, from_b0 = lax.optimization_barrier((*parts1, from_a0, from_b0))
    r1 = swapped(parts1[3], "rep", a_bit), swapped(parts1[4], "rep", b_bit)
    returned0 = to_planes(parts0[0], from_a0, from_b0)
    to_a1, to_b1 = reduced(parts1, r1)
    from_a1, from_b1 = swapped(to_a1, "rep", a_bit), swapped(to_b1, "rep", b_bit)
    returned = [returned0, to_planes(parts1[0], from_a1, from_b1)]

    pieces_back = [returned[c][s] for s in range(n_exp) for c in range(CHUNKS)]
    mine, send = combine(gate, embedded, pieces_back)
    other = swapped(send, "rep", 1 << CORE)
    return (mine + other.astype(F32)).astype(BF16)


def solution(mesh):
    return jax.shard_map(
        on_device,
        mesh=mesh,
        in_specs=(
            P(("rep", "exp"), None),
            P(),
            P(),
            P(("rep", "exp"), None),
            P(("rep", "exp"), None),
            P("exp", None, "rep"),
            P("exp", None, "rep"),
        ),
        out_specs=P(("rep", "exp"), None),
        check_vma=False,
    )
```

```python
import functools

import jax
import jax.numpy as jnp
from jax import lax
from jax.experimental import pallas as pl
from jax.experimental.pallas import tpu as pltpu
from jax.sharding import PartitionSpec as P

F32 = jnp.float32
BF16 = jnp.bfloat16
CHUNKS = 2
CORE, NEAR_A, NEAR_B = 0, 1, 2
GROUP_BITS = 3
MIB = 1024 * 1024
VMEM_LIMIT = 20 * MIB


def swapped(array, axis, distance):
    return lax.ppermute(array, axis, [(i, i ^ distance) for i in range(lax.axis_size(axis))])


def after(value, *others):
    return lax.optimization_barrier((value, *others))[0]


def mm(a, b, dims=((1,), (0,))):
    return lax.dot_general(a, b, (dims, ((), ())), preferred_element_type=F32)


def vmem():
    return pl.BlockSpec(memory_space=pltpu.VMEM)


def hbm():
    return pl.BlockSpec(memory_space=pltpu.HBM)


def in_hbm(array):
    return pltpu.with_memory_space_constraint(array, pltpu.HBM)


def in_vmem(array):
    return pltpu.with_memory_space_constraint(array, pltpu.VMEM)


def smem():
    return pl.BlockSpec(memory_space=pltpu.SMEM)


def embed_kernel(tubelets_ref, weight_ref, gain_ref, emb_ref, normed_ref):
    embedded = mm(tubelets_ref[...], weight_ref[...]).astype(BF16)
    emb_ref[...] = embedded
    floats = embedded.astype(F32)
    centred = floats - jnp.mean(floats, axis=-1, keepdims=True)
    variance = jnp.mean(centred * centred, axis=-1, keepdims=True)
    normed_ref[...] = (centred * lax.rsqrt(variance + 1e-06) * gain_ref[...]).astype(BF16)


def embed(tubelets, weight, gain):
    tok, width = tubelets.shape[0], weight.shape[1]
    shape = jax.ShapeDtypeStruct((tok, width), BF16)
    return pl.pallas_call(
        embed_kernel,
        out_shape=[shape, shape],
        in_specs=[vmem()] * 3,
        out_specs=[vmem()] * 2,
        compiler_params=pltpu.CompilerParams(vmem_limit_bytes=VMEM_LIMIT),
        cost_estimate=pl.CostEstimate(flops=2 * tok * weight.size, bytes_accessed=weight.size * 2, transcendentals=0),
        name="embed",
    )(tubelets, weight, gain.reshape(1, width))


def route_kernel(n_exp, half, cap, place_ref, code_ref, sib_code_ref, select_ref, gate_ref):
    tok = code_ref.shape[1]
    both = 2 * tok
    count = n_exp * half
    slots = 2 * cap
    rows = count * slots
    codes = jnp.concatenate([code_ref[...], sib_code_ref[...]], axis=1)
    gates = 0.25 + 0.125 * codes[2:4].astype(F32)
    plane, core = place_ref[0], place_ref[1]

    row = lax.broadcasted_iota(jnp.int32, (count, both), 0)
    expert = (plane ^ (row // half)) * (2 * half) + core * half + row % half
    first = codes[0:1] == expert
    second = codes[1:2] == expert
    member = first | second
    gated = jnp.where(first, gates[0:1, :], 0.0) + jnp.where(second, gates[1:2, :], 0.0)
    earlier = lax.broadcasted_iota(jnp.int32, (both, both), 0)
    later = lax.broadcasted_iota(jnp.int32, (both, both), 1)
    before = jnp.where(((earlier // tok) == (later // tok)) & (earlier < later), 1.0, 0.0).astype(BF16)
    rank = mm(jnp.where(member, 1.0, 0.0).astype(BF16), before)
    block = jnp.where(lax.broadcasted_iota(jnp.int32, (count, both), 1) >= tok, float(cap), 0.0)
    pos = jnp.where(member, rank + block, -1.0).astype(BF16)
    spread = jnp.where(
        lax.broadcasted_iota(jnp.int32, (rows, count), 0) // slots
        == lax.broadcasted_iota(jnp.int32, (rows, count), 1), 1.0, 0.0).astype(BF16)
    slot = (lax.broadcasted_iota(jnp.int32, (rows, both), 0) % slots).astype(F32)
    chosen = mm(spread, pos) == slot
    select_ref[...] = jnp.where(chosen, 1.0, 0.0).astype(BF16)
    gate_ref[...] = jnp.where(chosen, mm(spread, gated.astype(BF16)), 0.0).astype(BF16)


def route(place, codes, sib_codes, n_exp, half, cap):
    both = 2 * codes.shape[1]
    rows = n_exp * half * 2 * cap
    shape = jax.ShapeDtypeStruct((rows, both), BF16)
    return pl.pallas_call(
        functools.partial(route_kernel, n_exp, half, cap),
        out_shape=[shape, shape],
        in_specs=[smem()] + [vmem()] * 2,
        out_specs=[vmem()] * 2,
        compiler_params=pltpu.CompilerParams(vmem_limit_bytes=VMEM_LIMIT),
        cost_estimate=pl.CostEstimate(flops=2 * rows * both * 64, bytes_accessed=rows * both * 4, transcendentals=0),
        name="route",
    )(place, codes, sib_codes)


def pack_kernel(spans, select_ref, normed_ref, sib_ref, *piece_refs):
    buffer = mm(select_ref[...], jnp.concatenate([normed_ref[...], sib_ref[...]], axis=0))
    slots = piece_refs[0].shape[1]
    for (start, count), ref in zip(spans, piece_refs):
        for e in range(count):
            ref[e] = buffer[(start + e) * slots:(start + e + 1) * slots].astype(BF16)


def pack(select, normed, sib_normed, n_exp, half, cap):
    width = normed.shape[1]
    rows = select.shape[0]
    per = half // CHUNKS
    spans = []
    for s in range(n_exp):
        spans += [(s * half, half)] if s == 1 else [(s * half + c * per, per) for c in range(CHUNKS)]
    pieces = list(pl.pallas_call(
        functools.partial(pack_kernel, spans),
        out_shape=[pltpu.VMEM((count, 2 * cap, width), BF16) for _, count in spans],
        in_specs=[vmem()] * 3,
        out_specs=[vmem()] * len(spans),
        compiler_params=pltpu.CompilerParams(vmem_limit_bytes=VMEM_LIMIT),
        cost_estimate=pl.CostEstimate(
            flops=2 * select.size * width, bytes_accessed=rows * width * 4, transcendentals=0),
        name="pack",
    )(select, normed, sib_normed))
    return [[pieces.pop(0)] if s == 1 else [pieces.pop(0) for _ in range(CHUNKS)] for s in range(n_exp)]


def experts_kernel(chunk, half, place_ref, own_ref, a_ref, b_ref, d1_ref, d2_ref,
                   in_sib_ref, down_sib_ref, in_ref, down_ref,
                   p_own_ref, p_a_ref, p_b_ref, p_d1_ref, p_d2_ref, x_ref, h_ref, acc_ref, bufs, sems):
    per, m, _ = own_ref.shape
    split = per // 2
    base = place_ref[1] * half + chunk * per
    width = in_ref.shape[1]
    parts = sems.shape[2]
    depth = width // parts
    copies = {}
    for e in range(per):
        for which, ref in enumerate((in_ref, down_ref)):
            for part in range(parts):
                rows = pl.ds(part * depth, depth)
                copy = pltpu.make_async_copy(ref.at[base + e, rows], bufs.at[which, e, rows], sems.at[which, e, part])
                copy.start()
                copies[which, e, part] = copy

    def ready(which, e):
        for part in range(parts):
            copies[which, e, part].wait()

    for e in range(per):
        diagonal = d1_ref if e < split else d2_ref
        x_ref[e] = jnp.concatenate([own_ref[e], a_ref[e], b_ref[e], diagonal[e % split]], axis=0)
        h_ref[...] = jax.nn.gelu(mm(x_ref[e], in_sib_ref[base + e])).astype(BF16)
        acc_ref[e] = mm(h_ref[...], down_sib_ref[base + e], ((1,), (1,)))
    for e in range(per):
        p_diagonal = p_d1_ref if e < split else p_d2_ref
        ready(0, e)
        h_ref[...] = jax.nn.gelu(mm(x_ref[e], bufs[0, e])).astype(BF16)
        ready(1, e)
        total = acc_ref[e] + mm(h_ref[...], bufs[1, e], ((1,), (1,)))
        p_own_ref[e] = total[0:m].astype(BF16)
        p_a_ref[e] = total[m:2 * m].astype(BF16)
        p_b_ref[e] = total[2 * m:3 * m].astype(BF16)
        p_diagonal[e % split] = total[3 * m:4 * m].astype(BF16)


def experts(place, chunk, own, near_a, near_b, d1, d2, in_sib, down_sib, w_in, w_down):
    per, m, width = own.shape
    half, ff = in_sib.shape[0] // 2, in_sib.shape[2]
    shape = pltpu.VMEM(own.shape, BF16)
    part = pltpu.VMEM(d1.shape, BF16)
    return pl.pallas_call(
        functools.partial(experts_kernel, chunk, half),
        out_shape=[shape, shape, shape, part, part],
        in_specs=[smem()] + [vmem()] * 7 + [hbm()] * 2,
        out_specs=[vmem()] * 5,
        scratch_shapes=[
            pltpu.VMEM((per, 4 * m, width), BF16), pltpu.VMEM((4 * m, ff), BF16), pltpu.VMEM((per, 4 * m, width), F32),
            pltpu.VMEM((2, per, width, ff), BF16), pltpu.SemaphoreType.DMA((2, per, 4))],
        compiler_params=pltpu.CompilerParams(vmem_limit_bytes=VMEM_LIMIT),
        cost_estimate=pl.CostEstimate(
            flops=2 * per * 4 * m * width * 2 * ff * 2, bytes_accessed=per * m * width * 16,
            transcendentals=per * 4 * m * 2 * ff),
        name="experts",
    )(place, own, near_a, near_b, d1, d2, in_vmem(in_sib), in_vmem(down_sib), in_hbm(w_in), in_hbm(w_down))


def combine_kernel(tok, gate_ref, emb_ref, *refs):
    piece_refs, (mine_ref, send_ref, rows_ref) = refs[:-3], refs[-3:]
    per, slots, _ = piece_refs[0].shape
    for index, ref in enumerate(piece_refs):
        for e in range(per):
            start = (index * per + e) * slots
            rows_ref[start:start + slots] = ref[e].astype(F32)
    total = mm(gate_ref[...], rows_ref[...].astype(BF16), ((0,), (0,)))
    mine_ref[...] = total[0:tok] + emb_ref[...].astype(F32)
    send_ref[...] = total[tok:2 * tok].astype(BF16)


def combine(gate, embedded, pieces):
    tok, width = embedded.shape
    rows = gate.shape[0]
    return pl.pallas_call(
        functools.partial(combine_kernel, tok),
        out_shape=[jax.ShapeDtypeStruct((tok, width), F32), jax.ShapeDtypeStruct((tok, width), BF16)],
        in_specs=[vmem()] * (2 + len(pieces)),
        out_specs=[vmem()] * 2,
        scratch_shapes=[pltpu.VMEM((rows, width), F32)],
        compiler_params=pltpu.CompilerParams(vmem_limit_bytes=VMEM_LIMIT),
        cost_estimate=pl.CostEstimate(flops=4 * tok * rows * width, bytes_accessed=rows * width * 2, transcendentals=0),
        name="combine",
    )(gate, embedded, *pieces)


def on_device(tubelets, embed_weight, norm_gain, routes, gate_codes, w_in, w_down):
    tok = tubelets.shape[0]
    n_exp = lax.axis_size("exp")
    half = w_in.shape[0] // 2
    cap = 3 * tok // (w_in.shape[0] * n_exp)
    position = lax.axis_index("rep")
    core = position % 2
    place = jnp.stack([lax.axis_index("exp"), core]).astype(jnp.int32)

    core_bit = 1 << CORE
    codes = jnp.concatenate([routes.T, gate_codes.T], axis=0)
    sib_codes = swapped(codes, "rep", core_bit)
    embedded, normed = embed(tubelets, embed_weight, norm_gain)
    sib_normed = swapped(normed, "rep", core_bit)
    select, gate = route(place, codes, sib_codes, n_exp, half, cap)

    for bit in range(GROUP_BITS, lax.axis_size("rep").bit_length() - 1):
        upper = position // (1 << bit) % 2 == 1

        def gathered(panel):
            partner = swapped(panel, "rep", 1 << bit)
            return jnp.where(upper, jnp.concatenate([partner, panel], axis=2), jnp.concatenate([panel, partner], axis=2))

        w_in, w_down = gathered(w_in), gathered(w_down)

    in_sib = swapped(after(w_in, sib_normed, select), "rep", core_bit)
    down_sib = swapped(after(w_down, sib_normed, select), "rep", core_bit)
    pieces = pack(select, normed, sib_normed, n_exp, half, cap)

    def to_planes(p_own, from_a, from_b):
        done = (p_own.astype(F32) + from_a.astype(F32) + from_b.astype(F32)).astype(BF16)
        done = done.reshape(done.shape[0], n_exp, 2 * cap, done.shape[2])
        return [done[:, 0]] + [swapped(done[:, s], "exp", s) for s in range(1, n_exp)]

    split = half // CHUNKS // 2
    a_bit, b_bit = 1 << NEAR_A, 1 << NEAR_B

    def reduced(parts, r):
        _, p_a, p_b, _, _ = parts
        to_b = jnp.concatenate([p_b[:split] + r[0], p_b[split:]], axis=0)
        to_a = jnp.concatenate([p_a[:split], p_a[split:] + r[1]], axis=0)
        return to_a, to_b

    per = half // CHUNKS
    first = swapped(pieces[1][0], "exp", 1)
    own0 = jnp.concatenate(
        [pieces[0][0], first[:per]] + [swapped(pieces[s][0], "exp", s) for s in range(2, n_exp)], axis=1)
    late = lax.optimization_barrier((own0, in_sib, *(pieces[s][1] for s in range(2, n_exp))))[2:]
    own1 = jnp.concatenate(
        [pieces[0][1], first[per:]] + [swapped(piece, "exp", s + 2) for s, piece in enumerate(late)], axis=1)
    a0, b0 = swapped(own0, "rep", a_bit), swapped(own0, "rep", b_bit)
    own1 = after(own1, a0, b0)
    d0 = swapped(a0[:split], "rep", b_bit), swapped(b0[split:], "rep", a_bit)
    a1, b1 = swapped(own1, "rep", a_bit), swapped(own1, "rep", b_bit)
    parts0 = experts(place, 0, own0, a0, b0, *d0, in_sib, down_sib, w_in, w_down)
    a1, b1, *parts0 = lax.optimization_barrier((a1, b1, *parts0))
    d1 = swapped(a1[:split], "rep", b_bit), swapped(b1[split:], "rep", a_bit)
    r0 = swapped(parts0[3], "rep", a_bit), swapped(parts0[4], "rep", b_bit)
    to_a0, to_b0 = reduced(parts0, r0)
    to_a0, to_b0, *d1 = lax.optimization_barrier((to_a0, to_b0, *d1))
    from_a0, from_b0 = swapped(to_a0, "rep", a_bit), swapped(to_b0, "rep", b_bit)
    parts1 = experts(place, 1, own1, a1, b1, *d1, in_sib, down_sib, w_in, w_down)
    *parts1, from_a0, from_b0 = lax.optimization_barrier((*parts1, from_a0, from_b0))
    r1 = swapped(parts1[3], "rep", a_bit), swapped(parts1[4], "rep", b_bit)
    returned0 = to_planes(parts0[0], from_a0, from_b0)
    to_a1, to_b1 = reduced(parts1, r1)
    from_a1, from_b1 = swapped(to_a1, "rep", a_bit), swapped(to_b1, "rep", b_bit)
    returned = [returned0, to_planes(parts1[0], from_a1, from_b1)]

    pieces_back = [returned[c][s] for s in range(n_exp) for c in range(CHUNKS)]
    mine, send = combine(gate, embedded, pieces_back)
    other = swapped(send, "rep", 1 << CORE)
    return (mine + other.astype(F32)).astype(BF16)


def solution(mesh):
    return jax.shard_map(
        on_device,
        mesh=mesh,
        in_specs=(
            P(("rep", "exp"), None),
            P(),
            P(),
            P(("rep", "exp"), None),
            P(("rep", "exp"), None),
            P("exp", None, "rep"),
            P("exp", None, "rep"),
        ),
        out_specs=P(("rep", "exp"), None),
        check_vma=False,
    )
```

```python
import functools

import jax
import jax.numpy as jnp
from jax import lax
from jax.experimental import pallas as pl
from jax.experimental.pallas import tpu as pltpu
from jax.sharding import PartitionSpec as P

F32 = jnp.float32
BF16 = jnp.bfloat16
CHUNKS = 2
CORE, NEAR_A, NEAR_B = 0, 1, 2
GROUP_BITS = 3
MIB = 1024 * 1024
VMEM_LIMIT = 20 * MIB


def swapped(array, axis, distance):
    return lax.ppermute(array, axis, [(i, i ^ distance) for i in range(lax.axis_size(axis))])


def after(value, *others):
    return lax.optimization_barrier((value, *others))[0]


def mm(a, b, dims=((1,), (0,))):
    return lax.dot_general(a, b, (dims, ((), ())), preferred_element_type=F32)


def vmem():
    return pl.BlockSpec(memory_space=pltpu.VMEM)


def hbm():
    return pl.BlockSpec(memory_space=pltpu.HBM)


def in_hbm(array):
    return pltpu.with_memory_space_constraint(array, pltpu.HBM)


def in_vmem(array):
    return pltpu.with_memory_space_constraint(array, pltpu.VMEM)


def smem():
    return pl.BlockSpec(memory_space=pltpu.SMEM)


def embed_kernel(tubelets_ref, weight_ref, gain_ref, emb_ref, normed_ref, tub, weight, gain, sems):
    parts = sems.shape[0] - 2
    depth = weight_ref.shape[0] // parts
    copies = []
    for k in range(parts):
        rows = pl.ds(k * depth, depth)
        copies.append(pltpu.make_async_copy(weight_ref.at[rows], weight.at[rows], sems.at[k]))
    tub_copy = pltpu.make_async_copy(tubelets_ref, tub, sems.at[parts])
    gain_copy = pltpu.make_async_copy(gain_ref, gain, sems.at[parts + 1])
    for copy in (tub_copy, *copies, gain_copy):
        copy.start()
    tub_copy.wait()
    total = None
    for k in range(parts):
        copies[k].wait()
        rows = slice(k * depth, (k + 1) * depth)
        term = mm(tub[:, rows], weight[rows, :])
        total = term if total is None else total + term
    embedded = total.astype(BF16)
    emb_ref[...] = embedded
    floats = embedded.astype(F32)
    centred = floats - jnp.mean(floats, axis=-1, keepdims=True)
    variance = jnp.mean(centred * centred, axis=-1, keepdims=True)
    gain_copy.wait()
    normed_ref[...] = (centred * lax.rsqrt(variance + 1e-06) * gain[...]).astype(BF16)


def embed(tubelets, weight, gain):
    tok, width = tubelets.shape[0], weight.shape[1]
    parts = 6
    shape = pltpu.VMEM((tok, width), BF16)
    return pl.pallas_call(
        embed_kernel,
        out_shape=[shape, shape],
        in_specs=[hbm()] * 3,
        out_specs=[vmem()] * 2,
        scratch_shapes=[pltpu.VMEM(tubelets.shape, BF16), pltpu.VMEM(weight.shape, BF16),
                        pltpu.VMEM((1, width), F32), pltpu.SemaphoreType.DMA((parts + 2,))],
        compiler_params=pltpu.CompilerParams(vmem_limit_bytes=VMEM_LIMIT),
        cost_estimate=pl.CostEstimate(flops=2 * tok * weight.size, bytes_accessed=weight.size * 2, transcendentals=0),
        name="embed",
    )(in_hbm(tubelets), in_hbm(weight), in_hbm(gain.reshape(1, width)))


def route_kernel(n_exp, half, cap, place_ref, code_ref, sib_code_ref, select_ref, gate_ref):
    tok = code_ref.shape[1]
    both = 2 * tok
    count = n_exp * half
    slots = 2 * cap
    rows = count * slots
    codes = jnp.concatenate([code_ref[...], sib_code_ref[...]], axis=1)
    gates = 0.25 + 0.125 * codes[2:4].astype(F32)
    plane, core = place_ref[0], place_ref[1]

    row = lax.broadcasted_iota(jnp.int32, (count, both), 0)
    expert = (plane ^ (row // half)) * (2 * half) + core * half + row % half
    first = codes[0:1] == expert
    second = codes[1:2] == expert
    member = first | second
    gated = jnp.where(first, gates[0:1, :], 0.0) + jnp.where(second, gates[1:2, :], 0.0)
    earlier = lax.broadcasted_iota(jnp.int32, (both, both), 0)
    later = lax.broadcasted_iota(jnp.int32, (both, both), 1)
    before = jnp.where(((earlier // tok) == (later // tok)) & (earlier < later), 1.0, 0.0).astype(BF16)
    rank = mm(jnp.where(member, 1.0, 0.0).astype(BF16), before)
    block = jnp.where(lax.broadcasted_iota(jnp.int32, (count, both), 1) >= tok, float(cap), 0.0)
    pos = jnp.where(member, rank + block, -1.0).astype(BF16)
    spread = jnp.where(
        lax.broadcasted_iota(jnp.int32, (rows, count), 0) // slots
        == lax.broadcasted_iota(jnp.int32, (rows, count), 1), 1.0, 0.0).astype(BF16)
    slot = (lax.broadcasted_iota(jnp.int32, (rows, both), 0) % slots).astype(F32)
    chosen = mm(spread, pos) == slot
    select_ref[...] = jnp.where(chosen, 1.0, 0.0).astype(BF16)
    gate_ref[...] = jnp.where(chosen, mm(spread, gated.astype(BF16)), 0.0).astype(BF16)


def route(place, codes, sib_codes, n_exp, half, cap):
    both = 2 * codes.shape[1]
    rows = n_exp * half * 2 * cap
    shape = jax.ShapeDtypeStruct((rows, both), BF16)
    return pl.pallas_call(
        functools.partial(route_kernel, n_exp, half, cap),
        out_shape=[shape, shape],
        in_specs=[smem()] + [vmem()] * 2,
        out_specs=[vmem()] * 2,
        compiler_params=pltpu.CompilerParams(vmem_limit_bytes=VMEM_LIMIT),
        cost_estimate=pl.CostEstimate(flops=2 * rows * both * 64, bytes_accessed=rows * both * 4, transcendentals=0),
        name="route",
    )(place, codes, sib_codes)


def pack_kernel(spans, select_ref, normed_ref, sib_ref, *piece_refs):
    buffer = mm(select_ref[...], jnp.concatenate([normed_ref[...], sib_ref[...]], axis=0))
    slots = piece_refs[0].shape[1]
    for (start, count), ref in zip(spans, piece_refs):
        for e in range(count):
            ref[e] = buffer[(start + e) * slots:(start + e + 1) * slots].astype(BF16)


def pack(select, normed, sib_normed, n_exp, half, cap):
    width = normed.shape[1]
    rows = select.shape[0]
    per = half // CHUNKS
    spans = []
    for s in range(n_exp):
        spans += [(s * half, half)] if s == 1 else [(s * half + c * per, per) for c in range(CHUNKS)]
    pieces = list(pl.pallas_call(
        functools.partial(pack_kernel, spans),
        out_shape=[pltpu.VMEM((count, 2 * cap, width), BF16) for _, count in spans],
        in_specs=[vmem()] * 3,
        out_specs=[vmem()] * len(spans),
        compiler_params=pltpu.CompilerParams(vmem_limit_bytes=VMEM_LIMIT),
        cost_estimate=pl.CostEstimate(
            flops=2 * select.size * width, bytes_accessed=rows * width * 4, transcendentals=0),
        name="pack",
    )(select, normed, sib_normed))
    return [[pieces.pop(0)] if s == 1 else [pieces.pop(0) for _ in range(CHUNKS)] for s in range(n_exp)]


def experts_kernel(chunk, half, place_ref, own_ref, a_ref, b_ref, d1_ref, d2_ref,
                   in_sib_ref, down_sib_ref, in_ref, down_ref,
                   p_own_ref, p_a_ref, p_b_ref, p_d1_ref, p_d2_ref, x_ref, h_ref, acc_ref, bufs, sems):
    per, m, _ = own_ref.shape
    split = per // 2
    base = place_ref[1] * half + chunk * per
    width = in_ref.shape[1]
    parts = sems.shape[2]
    depth = width // parts
    copies = {}
    for e in range(per):
        for which, ref in enumerate((in_ref, down_ref)):
            for part in range(parts):
                rows = pl.ds(part * depth, depth)
                copy = pltpu.make_async_copy(ref.at[base + e, rows], bufs.at[which, e, rows], sems.at[which, e, part])
                copy.start()
                copies[which, e, part] = copy

    def ready(which, e):
        for part in range(parts):
            copies[which, e, part].wait()

    for e in range(per):
        diagonal = d1_ref if e < split else d2_ref
        x_ref[e] = jnp.concatenate([own_ref[e], a_ref[e], b_ref[e], diagonal[e % split]], axis=0)
        h_ref[...] = jax.nn.gelu(mm(x_ref[e], in_sib_ref[base + e])).astype(BF16)
        acc_ref[e] = mm(h_ref[...], down_sib_ref[base + e], ((1,), (1,)))
    for e in range(per):
        p_diagonal = p_d1_ref if e < split else p_d2_ref
        ready(0, e)
        h_ref[...] = jax.nn.gelu(mm(x_ref[e], bufs[0, e])).astype(BF16)
        ready(1, e)
        total = acc_ref[e] + mm(h_ref[...], bufs[1, e], ((1,), (1,)))
        p_own_ref[e] = total[0:m].astype(BF16)
        p_a_ref[e] = total[m:2 * m].astype(BF16)
        p_b_ref[e] = total[2 * m:3 * m].astype(BF16)
        p_diagonal[e % split] = total[3 * m:4 * m].astype(BF16)


def experts(place, chunk, own, near_a, near_b, d1, d2, in_sib, down_sib, w_in, w_down):
    per, m, width = own.shape
    half, ff = in_sib.shape[0] // 2, in_sib.shape[2]
    shape = pltpu.VMEM(own.shape, BF16)
    part = pltpu.VMEM(d1.shape, BF16)
    return pl.pallas_call(
        functools.partial(experts_kernel, chunk, half),
        out_shape=[shape, shape, shape, part, part],
        in_specs=[smem()] + [vmem()] * 7 + [hbm()] * 2,
        out_specs=[vmem()] * 5,
        scratch_shapes=[
            pltpu.VMEM((per, 4 * m, width), BF16), pltpu.VMEM((4 * m, ff), BF16), pltpu.VMEM((per, 4 * m, width), F32),
            pltpu.VMEM((2, per, width, ff), BF16), pltpu.SemaphoreType.DMA((2, per, 4))],
        compiler_params=pltpu.CompilerParams(vmem_limit_bytes=VMEM_LIMIT),
        cost_estimate=pl.CostEstimate(
            flops=2 * per * 4 * m * width * 2 * ff * 2, bytes_accessed=per * m * width * 16,
            transcendentals=per * 4 * m * 2 * ff),
        name="experts",
    )(place, own, near_a, near_b, d1, d2, in_vmem(in_sib), in_vmem(down_sib), in_hbm(w_in), in_hbm(w_down))


def combine_kernel(tok, gate_ref, emb_ref, *refs):
    piece_refs, (mine_ref, send_ref, rows_ref) = refs[:-3], refs[-3:]
    per, slots, _ = piece_refs[0].shape
    for index, ref in enumerate(piece_refs):
        for e in range(per):
            start = (index * per + e) * slots
            rows_ref[start:start + slots] = ref[e].astype(F32)
    total = mm(gate_ref[...], rows_ref[...].astype(BF16), ((0,), (0,)))
    mine_ref[...] = total[0:tok] + emb_ref[...].astype(F32)
    send_ref[...] = total[tok:2 * tok].astype(BF16)


def combine(gate, embedded, pieces):
    tok, width = embedded.shape
    rows = gate.shape[0]
    return pl.pallas_call(
        functools.partial(combine_kernel, tok),
        out_shape=[jax.ShapeDtypeStruct((tok, width), F32), jax.ShapeDtypeStruct((tok, width), BF16)],
        in_specs=[vmem()] * (2 + len(pieces)),
        out_specs=[vmem()] * 2,
        scratch_shapes=[pltpu.VMEM((rows, width), F32)],
        compiler_params=pltpu.CompilerParams(vmem_limit_bytes=VMEM_LIMIT),
        cost_estimate=pl.CostEstimate(flops=4 * tok * rows * width, bytes_accessed=rows * width * 2, transcendentals=0),
        name="combine",
    )(gate, embedded, *pieces)


def on_device(tubelets, embed_weight, norm_gain, routes, gate_codes, w_in, w_down):
    tok = tubelets.shape[0]
    n_exp = lax.axis_size("exp")
    half = w_in.shape[0] // 2
    cap = 3 * tok // (w_in.shape[0] * n_exp)
    position = lax.axis_index("rep")
    core = position % 2
    place = jnp.stack([lax.axis_index("exp"), core]).astype(jnp.int32)

    core_bit = 1 << CORE
    codes = jnp.concatenate([routes.T, gate_codes.T], axis=0)
    sib_codes = swapped(codes, "rep", core_bit)
    embedded, normed = embed(after(tubelets, codes), embed_weight, norm_gain)
    sib_normed = swapped(normed, "rep", core_bit)
    select, gate = route(place, codes, sib_codes, n_exp, half, cap)

    for bit in range(GROUP_BITS, lax.axis_size("rep").bit_length() - 1):
        upper = position // (1 << bit) % 2 == 1

        def gathered(panel):
            partner = swapped(panel, "rep", 1 << bit)
            return jnp.where(upper, jnp.concatenate([partner, panel], axis=2), jnp.concatenate([panel, partner], axis=2))

        w_in, w_down = gathered(w_in), gathered(w_down)

    in_sib = swapped(after(w_in, sib_normed, select), "rep", core_bit)
    down_sib = swapped(after(w_down, sib_normed, select), "rep", core_bit)
    pieces = pack(select, normed, sib_normed, n_exp, half, cap)

    def to_planes(p_own, from_a, from_b):
        done = (p_own.astype(F32) + from_a.astype(F32) + from_b.astype(F32)).astype(BF16)
        done = done.reshape(done.shape[0], n_exp, 2 * cap, done.shape[2])
        return [done[:, 0]] + [swapped(done[:, s], "exp", s) for s in range(1, n_exp)]

    split = half // CHUNKS // 2
    a_bit, b_bit = 1 << NEAR_A, 1 << NEAR_B

    def reduced(parts, r):
        _, p_a, p_b, _, _ = parts
        to_b = jnp.concatenate([p_b[:split] + r[0], p_b[split:]], axis=0)
        to_a = jnp.concatenate([p_a[:split], p_a[split:] + r[1]], axis=0)
        return to_a, to_b

    per = half // CHUNKS
    far0 = [swapped(pieces[s][0], "exp", s) for s in range(2, n_exp)]
    first = swapped(pieces[1][0], "exp", 1)
    own0 = jnp.concatenate([pieces[0][0], first[:per]] + far0, axis=1)
    late = lax.optimization_barrier((own0, in_sib, *(pieces[s][1] for s in range(2, n_exp))))[2:]
    own1 = jnp.concatenate(
        [pieces[0][1], first[per:]] + [swapped(piece, "exp", s + 2) for s, piece in enumerate(late)], axis=1)
    a0, b0 = swapped(own0, "rep", a_bit), swapped(own0, "rep", b_bit)
    own1 = after(own1, a0, b0)
    d0 = swapped(a0[:split], "rep", b_bit), swapped(b0[split:], "rep", a_bit)
    a1, b1 = swapped(own1, "rep", a_bit), swapped(own1, "rep", b_bit)
    parts0 = experts(place, 0, own0, a0, b0, *d0, in_sib, down_sib, w_in, w_down)
    a1, b1, *parts0 = lax.optimization_barrier((a1, b1, *parts0))
    d1 = swapped(a1[:split], "rep", b_bit), swapped(b1[split:], "rep", a_bit)
    r0 = swapped(parts0[3], "rep", a_bit), swapped(parts0[4], "rep", b_bit)
    to_a0, to_b0 = reduced(parts0, r0)
    to_a0, to_b0, *d1 = lax.optimization_barrier((to_a0, to_b0, *d1))
    from_a0, from_b0 = swapped(to_a0, "rep", a_bit), swapped(to_b0, "rep", b_bit)
    parts1 = experts(place, 1, own1, a1, b1, *d1, in_sib, down_sib, w_in, w_down)
    *parts1, from_a0, from_b0 = lax.optimization_barrier((*parts1, from_a0, from_b0))
    r1 = swapped(parts1[3], "rep", a_bit), swapped(parts1[4], "rep", b_bit)
    returned0 = to_planes(parts0[0], from_a0, from_b0)
    to_a1, to_b1 = reduced(parts1, r1)
    from_a1, from_b1 = swapped(to_a1, "rep", a_bit), swapped(to_b1, "rep", b_bit)
    returned = [returned0, to_planes(parts1[0], from_a1, from_b1)]

    pieces_back = [returned[c][s] for s in range(n_exp) for c in range(CHUNKS)]
    mine, send = combine(gate, embedded, pieces_back)
    other = swapped(send, "rep", 1 << CORE)
    return (mine + other.astype(F32)).astype(BF16)


def solution(mesh):
    return jax.shard_map(
        on_device,
        mesh=mesh,
        in_specs=(
            P(("rep", "exp"), None),
            P(),
            P(),
            P(("rep", "exp"), None),
            P(("rep", "exp"), None),
            P("exp", None, "rep"),
            P("exp", None, "rep"),
        ),
        out_specs=P(("rep", "exp"), None),
        check_vma=False,
    )
```

```python
import functools

import jax
import jax.numpy as jnp
from jax import lax
from jax.experimental import pallas as pl
from jax.experimental.pallas import tpu as pltpu
from jax.sharding import PartitionSpec as P

F32 = jnp.float32
BF16 = jnp.bfloat16
CHUNKS = 2
CORE, NEAR_A, NEAR_B = 0, 1, 2
GROUP_BITS = 3
MIB = 1024 * 1024
VMEM_LIMIT = 20 * MIB


def swapped(array, axis, distance):
    return lax.ppermute(array, axis, [(i, i ^ distance) for i in range(lax.axis_size(axis))])


def after(value, *others):
    return lax.optimization_barrier((value, *others))[0]


def mm(a, b, dims=((1,), (0,))):
    return lax.dot_general(a, b, (dims, ((), ())), preferred_element_type=F32)


def vmem():
    return pl.BlockSpec(memory_space=pltpu.VMEM)


def hbm():
    return pl.BlockSpec(memory_space=pltpu.HBM)


def in_hbm(array):
    return pltpu.with_memory_space_constraint(array, pltpu.HBM)


def in_vmem(array):
    return pltpu.with_memory_space_constraint(array, pltpu.VMEM)


def smem():
    return pl.BlockSpec(memory_space=pltpu.SMEM)


def embed_kernel(tubelets_ref, weight_ref, gain_ref, emb_ref, normed_ref, tub, weight, gain, sems):
    parts = sems.shape[0] - 2
    depth = weight_ref.shape[0] // parts
    copies = []
    for k in range(parts):
        rows = pl.ds(k * depth, depth)
        copies.append(pltpu.make_async_copy(weight_ref.at[rows], weight.at[rows], sems.at[k]))
    tub_copy = pltpu.make_async_copy(tubelets_ref, tub, sems.at[parts])
    gain_copy = pltpu.make_async_copy(gain_ref, gain, sems.at[parts + 1])
    for copy in (tub_copy, *copies, gain_copy):
        copy.start()
    tub_copy.wait()
    total = None
    for k in range(parts):
        copies[k].wait()
        rows = slice(k * depth, (k + 1) * depth)
        term = mm(tub[:, rows], weight[rows, :])
        total = term if total is None else total + term
    embedded = total.astype(BF16)
    emb_ref[...] = embedded
    floats = embedded.astype(F32)
    centred = floats - jnp.mean(floats, axis=-1, keepdims=True)
    variance = jnp.mean(centred * centred, axis=-1, keepdims=True)
    gain_copy.wait()
    normed_ref[...] = (centred * lax.rsqrt(variance + 1e-06) * gain[...]).astype(BF16)


def embed(tubelets, weight, gain):
    tok, width = tubelets.shape[0], weight.shape[1]
    parts = 6
    shape = pltpu.VMEM((tok, width), BF16)
    return pl.pallas_call(
        embed_kernel,
        out_shape=[shape, shape],
        in_specs=[hbm()] * 3,
        out_specs=[vmem()] * 2,
        scratch_shapes=[pltpu.VMEM(tubelets.shape, BF16), pltpu.VMEM(weight.shape, BF16),
                        pltpu.VMEM((1, width), F32), pltpu.SemaphoreType.DMA((parts + 2,))],
        compiler_params=pltpu.CompilerParams(vmem_limit_bytes=VMEM_LIMIT),
        cost_estimate=pl.CostEstimate(flops=2 * tok * weight.size, bytes_accessed=weight.size * 2, transcendentals=0),
        name="embed",
    )(in_hbm(tubelets), in_hbm(weight), in_hbm(gain.reshape(1, width)))


def route_kernel(n_exp, half, cap, place_ref, code_ref, sib_code_ref, select_ref, gate_ref):
    tok = code_ref.shape[1]
    both = 2 * tok
    count = n_exp * half
    slots = 2 * cap
    rows = count * slots
    codes = jnp.concatenate([code_ref[...], sib_code_ref[...]], axis=1)
    gates = 0.25 + 0.125 * codes[2:4].astype(F32)
    plane, core = place_ref[0], place_ref[1]

    row = lax.broadcasted_iota(jnp.int32, (count, both), 0)
    expert = (plane ^ (row // half)) * (2 * half) + core * half + row % half
    first = codes[0:1] == expert
    second = codes[1:2] == expert
    member = first | second
    gated = jnp.where(first, gates[0:1, :], 0.0) + jnp.where(second, gates[1:2, :], 0.0)
    earlier = lax.broadcasted_iota(jnp.int32, (both, both), 0)
    later = lax.broadcasted_iota(jnp.int32, (both, both), 1)
    before = jnp.where(((earlier // tok) == (later // tok)) & (earlier < later), 1.0, 0.0).astype(BF16)
    rank = mm(jnp.where(member, 1.0, 0.0).astype(BF16), before)
    block = jnp.where(lax.broadcasted_iota(jnp.int32, (count, both), 1) >= tok, float(cap), 0.0)
    pos = jnp.where(member, rank + block, -1.0).astype(BF16)
    spread = jnp.where(
        lax.broadcasted_iota(jnp.int32, (rows, count), 0) // slots
        == lax.broadcasted_iota(jnp.int32, (rows, count), 1), 1.0, 0.0).astype(BF16)
    slot = (lax.broadcasted_iota(jnp.int32, (rows, both), 0) % slots).astype(F32)
    chosen = mm(spread, pos) == slot
    select_ref[...] = jnp.where(chosen, 1.0, 0.0).astype(BF16)
    gate_ref[...] = jnp.where(chosen, mm(spread, gated.astype(BF16)), 0.0).astype(BF16)


def route(place, codes, sib_codes, n_exp, half, cap):
    both = 2 * codes.shape[1]
    rows = n_exp * half * 2 * cap
    shape = jax.ShapeDtypeStruct((rows, both), BF16)
    return pl.pallas_call(
        functools.partial(route_kernel, n_exp, half, cap),
        out_shape=[shape, shape],
        in_specs=[smem()] + [vmem()] * 2,
        out_specs=[vmem()] * 2,
        compiler_params=pltpu.CompilerParams(vmem_limit_bytes=VMEM_LIMIT),
        cost_estimate=pl.CostEstimate(flops=2 * rows * both * 64, bytes_accessed=rows * both * 4, transcendentals=0),
        name="route",
    )(place, codes, sib_codes)


def pack_kernel(spans, select_ref, normed_ref, sib_ref, *piece_refs):
    buffer = mm(select_ref[...], jnp.concatenate([normed_ref[...], sib_ref[...]], axis=0))
    slots = piece_refs[0].shape[1]
    for (start, count), ref in zip(spans, piece_refs):
        for e in range(count):
            ref[e] = buffer[(start + e) * slots:(start + e + 1) * slots].astype(BF16)


def pack(select, normed, sib_normed, n_exp, half, cap):
    width = normed.shape[1]
    rows = select.shape[0]
    per = half // CHUNKS
    spans = []
    for s in range(n_exp):
        spans += [(s * half, half)] if s == 1 else [(s * half + c * per, per) for c in range(CHUNKS)]
    pieces = list(pl.pallas_call(
        functools.partial(pack_kernel, spans),
        out_shape=[pltpu.VMEM((count, 2 * cap, width), BF16) for _, count in spans],
        in_specs=[vmem()] * 3,
        out_specs=[vmem()] * len(spans),
        compiler_params=pltpu.CompilerParams(vmem_limit_bytes=VMEM_LIMIT),
        cost_estimate=pl.CostEstimate(
            flops=2 * select.size * width, bytes_accessed=rows * width * 4, transcendentals=0),
        name="pack",
    )(select, normed, sib_normed))
    return [[pieces.pop(0)] if s == 1 else [pieces.pop(0) for _ in range(CHUNKS)] for s in range(n_exp)]


def hold_kernel(place_ref, in_ref, down_ref, in_out, down_out, sems):
    count = in_out.shape[0]
    copies = []
    for e in range(count):
        index = place_ref[1] * count + e
        for which, (source, target) in enumerate(((in_ref, in_out), (down_ref, down_out))):
            copies.append(pltpu.make_async_copy(source.at[index], target.at[e], sems.at[which, e]))
            copies[-1].start()
    for copy in copies:
        copy.wait()


def hold(place, w_in, w_down):
    shape = pltpu.VMEM((w_in.shape[0] // 2, *w_in.shape[1:]), BF16)
    return pl.pallas_call(
        hold_kernel,
        out_shape=[shape, shape],
        in_specs=[smem(), hbm(), hbm()],
        out_specs=[vmem()] * 2,
        scratch_shapes=[pltpu.SemaphoreType.DMA((2, w_in.shape[0] // 2))],
        compiler_params=pltpu.CompilerParams(vmem_limit_bytes=VMEM_LIMIT),
        cost_estimate=pl.CostEstimate(flops=0, bytes_accessed=w_in.size * 4, transcendentals=0),
        name="hold",
    )(place, in_hbm(w_in), in_hbm(w_down))


def experts_kernel(chunk, half, place_ref, own_ref, a_ref, b_ref, d1_ref, d2_ref,
                   in_own_ref, in_sib_ref, down_own_ref, down_sib_ref,
                   p_own_ref, p_a_ref, p_b_ref, p_d1_ref, p_d2_ref, h_ref):
    per, m, _ = own_ref.shape
    split = per // 2
    for e in range(per):
        mine = chunk * per + e
        index = place_ref[1] * half + mine
        diagonal, p_diagonal = (d1_ref, p_d1_ref) if e < split else (d2_ref, p_d2_ref)
        x = jnp.concatenate([own_ref[e], a_ref[e], b_ref[e], diagonal[e % split]], axis=0)
        h_ref[0] = jax.nn.gelu(mm(x, in_own_ref[mine])).astype(BF16)
        h_ref[1] = jax.nn.gelu(mm(x, in_sib_ref[index])).astype(BF16)
        total = mm(h_ref[0], down_own_ref[mine], ((1,), (1,))) + mm(h_ref[1], down_sib_ref[index], ((1,), (1,)))
        p_own_ref[e] = total[0:m].astype(BF16)
        p_a_ref[e] = total[m:2 * m].astype(BF16)
        p_b_ref[e] = total[2 * m:3 * m].astype(BF16)
        p_diagonal[e % split] = total[3 * m:4 * m].astype(BF16)


def experts(place, chunk, own, near_a, near_b, d1, d2, in_own, in_sib, down_own, down_sib):
    per, m, width = own.shape
    half, _, ff = in_own.shape
    shape = pltpu.VMEM(own.shape, BF16)
    part = pltpu.VMEM(d1.shape, BF16)
    return pl.pallas_call(
        functools.partial(experts_kernel, chunk, half),
        out_shape=[shape, shape, shape, part, part],
        in_specs=[smem()] + [vmem()] * 9,
        out_specs=[vmem()] * 5,
        scratch_shapes=[pltpu.VMEM((2, 4 * m, ff), BF16)],
        compiler_params=pltpu.CompilerParams(vmem_limit_bytes=VMEM_LIMIT),
        cost_estimate=pl.CostEstimate(
            flops=2 * per * 4 * m * width * 2 * ff * 2, bytes_accessed=per * m * width * 16,
            transcendentals=per * 4 * m * 2 * ff),
        name="experts",
    )(place, own, near_a, near_b, d1, d2, *(in_vmem(panel) for panel in (in_own, in_sib, down_own, down_sib)))


def combine_kernel(tok, gate_ref, emb_ref, *refs):
    piece_refs, (mine_ref, send_ref, rows_ref) = refs[:-3], refs[-3:]
    per, slots, _ = piece_refs[0].shape
    for index, ref in enumerate(piece_refs):
        for e in range(per):
            start = (index * per + e) * slots
            rows_ref[start:start + slots] = ref[e].astype(F32)
    total = mm(gate_ref[...], rows_ref[...].astype(BF16), ((0,), (0,)))
    mine_ref[...] = total[0:tok] + emb_ref[...].astype(F32)
    send_ref[...] = total[tok:2 * tok].astype(BF16)


def combine(gate, embedded, pieces):
    tok, width = embedded.shape
    rows = gate.shape[0]
    return pl.pallas_call(
        functools.partial(combine_kernel, tok),
        out_shape=[jax.ShapeDtypeStruct((tok, width), F32), jax.ShapeDtypeStruct((tok, width), BF16)],
        in_specs=[vmem()] * (2 + len(pieces)),
        out_specs=[vmem()] * 2,
        scratch_shapes=[pltpu.VMEM((rows, width), F32)],
        compiler_params=pltpu.CompilerParams(vmem_limit_bytes=VMEM_LIMIT),
        cost_estimate=pl.CostEstimate(flops=4 * tok * rows * width, bytes_accessed=rows * width * 2, transcendentals=0),
        name="combine",
    )(gate, embedded, *pieces)


def on_device(tubelets, embed_weight, norm_gain, routes, gate_codes, w_in, w_down):
    tok = tubelets.shape[0]
    n_exp = lax.axis_size("exp")
    half = w_in.shape[0] // 2
    cap = 3 * tok // (w_in.shape[0] * n_exp)
    position = lax.axis_index("rep")
    core = position % 2
    place = jnp.stack([lax.axis_index("exp"), core]).astype(jnp.int32)

    core_bit = 1 << CORE
    codes = jnp.concatenate([routes.T, gate_codes.T], axis=0)
    sib_codes = swapped(codes, "rep", core_bit)
    embedded, normed = embed(after(tubelets, codes), embed_weight, norm_gain)
    sib_normed = swapped(normed, "rep", core_bit)
    select, gate = route(place, codes, sib_codes, n_exp, half, cap)

    for bit in range(GROUP_BITS, lax.axis_size("rep").bit_length() - 1):
        upper = position // (1 << bit) % 2 == 1

        def gathered(panel):
            partner = swapped(panel, "rep", 1 << bit)
            return jnp.where(upper, jnp.concatenate([partner, panel], axis=2), jnp.concatenate([panel, partner], axis=2))

        w_in, w_down = gathered(w_in), gathered(w_down)

    in_sib = swapped(after(w_in, sib_normed, select), "rep", core_bit)
    down_sib = swapped(after(w_down, sib_normed, select), "rep", core_bit)
    pieces = pack(select, normed, sib_normed, n_exp, half, cap)

    def to_planes(p_own, from_a, from_b):
        done = (p_own.astype(F32) + from_a.astype(F32) + from_b.astype(F32)).astype(BF16)
        done = done.reshape(done.shape[0], n_exp, 2 * cap, done.shape[2])
        return [done[:, 0]] + [swapped(done[:, s], "exp", s) for s in range(1, n_exp)]

    split = half // CHUNKS // 2
    a_bit, b_bit = 1 << NEAR_A, 1 << NEAR_B

    def reduced(parts, r):
        _, p_a, p_b, _, _ = parts
        to_b = jnp.concatenate([p_b[:split] + r[0], p_b[split:]], axis=0)
        to_a = jnp.concatenate([p_a[:split], p_a[split:] + r[1]], axis=0)
        return to_a, to_b

    per = half // CHUNKS
    far0 = [swapped(pieces[s][0], "exp", s) for s in range(2, n_exp)]
    first = swapped(pieces[1][0], "exp", 1)
    in_own, down_own = hold(after(place, first), w_in, w_down)
    own0 = after(jnp.concatenate([pieces[0][0], first[:per]] + far0, axis=1), in_own)
    late = lax.optimization_barrier((own0, in_sib, *(pieces[s][1] for s in range(2, n_exp))))[2:]
    own1 = jnp.concatenate(
        [pieces[0][1], first[per:]] + [swapped(piece, "exp", s + 2) for s, piece in enumerate(late)], axis=1)
    a0, b0 = swapped(own0, "rep", a_bit), swapped(own0, "rep", b_bit)
    own1 = after(own1, a0, b0)
    d0 = swapped(a0[:split], "rep", b_bit), swapped(b0[split:], "rep", a_bit)
    a1, b1 = swapped(own1, "rep", a_bit), swapped(own1, "rep", b_bit)
    parts0 = experts(place, 0, own0, a0, b0, *d0, in_own, in_sib, down_own, down_sib)
    a1, b1, *parts0 = lax.optimization_barrier((a1, b1, *parts0))
    r0 = swapped(parts0[3], "rep", a_bit), swapped(parts0[4], "rep", b_bit)
    d1 = swapped(after(a1[:split], r0[0]), "rep", b_bit), swapped(b1[split:], "rep", a_bit)
    to_a0, to_b0 = reduced(parts0, r0)
    d1 = lax.optimization_barrier((*d1, to_a0, to_b0))[:2]
    from_a0, from_b0 = swapped(to_a0, "rep", a_bit), swapped(to_b0, "rep", b_bit)
    parts1 = list(experts(place, 1, own1, a1, b1, *d1, in_own, in_sib, down_own, down_sib))
    parts1[4] = after(parts1[4], from_a0, from_b0)
    r1 = swapped(parts1[3], "rep", a_bit), swapped(parts1[4], "rep", b_bit)
    returned0 = to_planes(parts0[0], from_a0, from_b0)
    to_a1, to_b1 = reduced(parts1, r1)
    from_a1, from_b1 = swapped(to_a1, "rep", a_bit), swapped(to_b1, "rep", b_bit)
    returned = [returned0, to_planes(parts1[0], from_a1, from_b1)]

    pieces_back = [returned[c][s] for s in range(n_exp) for c in range(CHUNKS)]
    mine, send = combine(gate, embedded, pieces_back)
    other = swapped(send, "rep", 1 << CORE)
    return (mine + other.astype(F32)).astype(BF16)


def solution(mesh):
    return jax.shard_map(
        on_device,
        mesh=mesh,
        in_specs=(
            P(("rep", "exp"), None),
            P(),
            P(),
            P(("rep", "exp"), None),
            P(("rep", "exp"), None),
            P("exp", None, "rep"),
            P("exp", None, "rep"),
        ),
        out_specs=P(("rep", "exp"), None),
        check_vma=False,
    )
```

```python
import functools

import jax
import jax.numpy as jnp
from jax import lax
from jax.experimental import pallas as pl
from jax.experimental.pallas import tpu as pltpu
from jax.sharding import PartitionSpec as P

F32 = jnp.float32
BF16 = jnp.bfloat16
CHUNKS = 2
CORE, NEAR_A, NEAR_B = 0, 1, 2
GROUP_BITS = 3
MIB = 1024 * 1024
VMEM_LIMIT = 20 * MIB


def swapped(array, axis, distance):
    return lax.ppermute(array, axis, [(i, i ^ distance) for i in range(lax.axis_size(axis))])


def after(value, *others):
    return lax.optimization_barrier((value, *others))[0]


def mm(a, b, dims=((1,), (0,))):
    return lax.dot_general(a, b, (dims, ((), ())), preferred_element_type=F32)


def vmem():
    return pl.BlockSpec(memory_space=pltpu.VMEM)


def hbm():
    return pl.BlockSpec(memory_space=pltpu.HBM)


def in_hbm(array):
    return pltpu.with_memory_space_constraint(array, pltpu.HBM)


def in_vmem(array):
    return pltpu.with_memory_space_constraint(array, pltpu.VMEM)


def smem():
    return pl.BlockSpec(memory_space=pltpu.SMEM)


def embed_kernel(tubelets_ref, weight_ref, gain_ref, emb_ref, normed_ref, tub, weight, gain, sems):
    parts = sems.shape[0] - 2
    depth = weight_ref.shape[0] // parts
    copies = []
    for k in range(parts):
        rows = pl.ds(k * depth, depth)
        copies.append(pltpu.make_async_copy(weight_ref.at[rows], weight.at[rows], sems.at[k]))
    tub_copy = pltpu.make_async_copy(tubelets_ref, tub, sems.at[parts])
    gain_copy = pltpu.make_async_copy(gain_ref, gain, sems.at[parts + 1])
    for copy in (tub_copy, *copies, gain_copy):
        copy.start()
    tub_copy.wait()
    total = None
    for k in range(parts):
        copies[k].wait()
        rows = slice(k * depth, (k + 1) * depth)
        term = mm(tub[:, rows], weight[rows, :])
        total = term if total is None else total + term
    embedded = total.astype(BF16)
    emb_ref[...] = embedded
    floats = embedded.astype(F32)
    centred = floats - jnp.mean(floats, axis=-1, keepdims=True)
    variance = jnp.mean(centred * centred, axis=-1, keepdims=True)
    gain_copy.wait()
    normed_ref[...] = (centred * lax.rsqrt(variance + 1e-06) * gain[...]).astype(BF16)


def embed(tubelets, weight, gain):
    tok, width = tubelets.shape[0], weight.shape[1]
    parts = 6
    shape = pltpu.VMEM((tok, width), BF16)
    return pl.pallas_call(
        embed_kernel,
        out_shape=[shape, shape],
        in_specs=[hbm()] * 3,
        out_specs=[vmem()] * 2,
        scratch_shapes=[pltpu.VMEM(tubelets.shape, BF16), pltpu.VMEM(weight.shape, BF16),
                        pltpu.VMEM((1, width), F32), pltpu.SemaphoreType.DMA((parts + 2,))],
        compiler_params=pltpu.CompilerParams(vmem_limit_bytes=VMEM_LIMIT),
        cost_estimate=pl.CostEstimate(flops=2 * tok * weight.size, bytes_accessed=weight.size * 2, transcendentals=0),
        name="embed",
    )(in_hbm(tubelets), in_hbm(weight), in_hbm(gain.reshape(1, width)))


def route_kernel(n_exp, half, cap, place_ref, code_ref, sib_code_ref, select_ref, gate_ref):
    tok = code_ref.shape[1]
    both = 2 * tok
    count = n_exp * half
    slots = 2 * cap
    rows = count * slots
    codes = jnp.concatenate([code_ref[...], sib_code_ref[...]], axis=1)
    gates = 0.25 + 0.125 * codes[2:4].astype(F32)
    plane, core = place_ref[0], place_ref[1]

    row = lax.broadcasted_iota(jnp.int32, (count, both), 0)
    expert = (plane ^ (row // half)) * (2 * half) + core * half + row % half
    first = codes[0:1] == expert
    second = codes[1:2] == expert
    member = first | second
    gated = jnp.where(first, gates[0:1, :], 0.0) + jnp.where(second, gates[1:2, :], 0.0)
    earlier = lax.broadcasted_iota(jnp.int32, (both, both), 0)
    later = lax.broadcasted_iota(jnp.int32, (both, both), 1)
    before = jnp.where(((earlier // tok) == (later // tok)) & (earlier < later), 1.0, 0.0).astype(BF16)
    rank = mm(jnp.where(member, 1.0, 0.0).astype(BF16), before)
    block = jnp.where(lax.broadcasted_iota(jnp.int32, (count, both), 1) >= tok, float(cap), 0.0)
    pos = jnp.where(member, rank + block, -1.0).astype(BF16)
    spread = jnp.where(
        lax.broadcasted_iota(jnp.int32, (rows, count), 0) // slots
        == lax.broadcasted_iota(jnp.int32, (rows, count), 1), 1.0, 0.0).astype(BF16)
    slot = (lax.broadcasted_iota(jnp.int32, (rows, both), 0) % slots).astype(F32)
    chosen = mm(spread, pos) == slot
    select_ref[...] = jnp.where(chosen, 1.0, 0.0).astype(BF16)
    gate_ref[...] = jnp.where(chosen, mm(spread, gated.astype(BF16)), 0.0).astype(BF16)


def route(place, codes, sib_codes, n_exp, half, cap):
    both = 2 * codes.shape[1]
    rows = n_exp * half * 2 * cap
    shape = jax.ShapeDtypeStruct((rows, both), BF16)
    return pl.pallas_call(
        functools.partial(route_kernel, n_exp, half, cap),
        out_shape=[shape, shape],
        in_specs=[smem()] + [vmem()] * 2,
        out_specs=[vmem()] * 2,
        compiler_params=pltpu.CompilerParams(vmem_limit_bytes=VMEM_LIMIT),
        cost_estimate=pl.CostEstimate(flops=2 * rows * both * 64, bytes_accessed=rows * both * 4, transcendentals=0),
        name="route",
    )(place, codes, sib_codes)


def pack_kernel(spans, select_ref, normed_ref, sib_ref, *piece_refs):
    buffer = mm(select_ref[...], jnp.concatenate([normed_ref[...], sib_ref[...]], axis=0))
    slots = piece_refs[0].shape[1]
    for (start, count), ref in zip(spans, piece_refs):
        for e in range(count):
            ref[e] = buffer[(start + e) * slots:(start + e + 1) * slots].astype(BF16)


def pack(select, normed, sib_normed, n_exp, half, cap):
    width = normed.shape[1]
    rows = select.shape[0]
    per = half // CHUNKS
    spans = []
    for s in range(n_exp):
        spans += [(s * half, half)] if s < 2 else [(s * half + c * per, per) for c in range(CHUNKS)]
    pieces = list(pl.pallas_call(
        functools.partial(pack_kernel, spans),
        out_shape=[pltpu.VMEM((count, 2 * cap, width), BF16) for _, count in spans],
        in_specs=[vmem()] * 3,
        out_specs=[vmem()] * len(spans),
        compiler_params=pltpu.CompilerParams(vmem_limit_bytes=VMEM_LIMIT),
        cost_estimate=pl.CostEstimate(
            flops=2 * select.size * width, bytes_accessed=rows * width * 4, transcendentals=0),
        name="pack",
    )(select, normed, sib_normed))
    return [[pieces.pop(0)] if s < 2 else [pieces.pop(0) for _ in range(CHUNKS)] for s in range(n_exp)]


def lend_kernel(place_ref, in_ref, down_ref, out_ref, sems):
    count = out_ref.shape[1]
    start = (1 - place_ref[1]) * count
    copies = []
    for e in range(count):
        for which, source in enumerate((in_ref, down_ref)):
            copies.append(pltpu.make_async_copy(source.at[start + e], out_ref.at[which, e], sems.at[which, e]))
            copies[-1].start()
    for copy in copies:
        copy.wait()


def lend(place, w_in, w_down):
    shape = (2, w_in.shape[0] // 2, *w_in.shape[1:])
    return pl.pallas_call(
        lend_kernel,
        out_shape=pltpu.VMEM(shape, BF16),
        in_specs=[smem(), hbm(), hbm()],
        out_specs=vmem(),
        scratch_shapes=[pltpu.SemaphoreType.DMA(shape[:2])],
        compiler_params=pltpu.CompilerParams(vmem_limit_bytes=VMEM_LIMIT),
        cost_estimate=pl.CostEstimate(flops=0, bytes_accessed=w_in.size * 4, transcendentals=0),
        name="lend",
    )(place, in_hbm(w_in), in_hbm(w_down))


def hold_kernel(place_ref, in_ref, down_ref, in_out, down_out, sems):
    count = in_out.shape[0]
    copies = []
    for e in range(count):
        index = place_ref[1] * count + e
        for which, (source, target) in enumerate(((in_ref, in_out), (down_ref, down_out))):
            copies.append(pltpu.make_async_copy(source.at[index], target.at[e], sems.at[which, e]))
            copies[-1].start()
    for copy in copies:
        copy.wait()


def hold(place, w_in, w_down):
    shape = pltpu.VMEM((w_in.shape[0] // 2, *w_in.shape[1:]), BF16)
    return pl.pallas_call(
        hold_kernel,
        out_shape=[shape, shape],
        in_specs=[smem(), hbm(), hbm()],
        out_specs=[vmem()] * 2,
        scratch_shapes=[pltpu.SemaphoreType.DMA((2, w_in.shape[0] // 2))],
        compiler_params=pltpu.CompilerParams(vmem_limit_bytes=VMEM_LIMIT),
        cost_estimate=pl.CostEstimate(flops=0, bytes_accessed=w_in.size * 4, transcendentals=0),
        name="hold",
    )(place, in_hbm(w_in), in_hbm(w_down))


def experts_kernel(chunk, *refs):
    rows_refs, (sib_ref, in_ref, down_ref), outs = refs[:9], refs[9:12], refs[12:21]
    h_ref = refs[21]
    per = rows_refs[0].shape[0]
    split = per // 2
    first = chunk * per
    def blocks(refs, e, whole):
        far, far_a, far_b, d1, d2, own, own_a, own_b, own_d = refs
        mine = first + e if whole else e
        diagonal = (d1, e) if e < split else (d2, e - split)
        return [(far, e), (far_a, e), (far_b, e), diagonal, (own, mine), (own_a, mine), (own_b, mine), (own_d, e)]

    for e in range(per):
        mine = first + e
        x = jnp.concatenate([ref[i] for ref, i in blocks(rows_refs, e, True)], axis=0)
        h_ref[0] = jax.nn.gelu(mm(x, in_ref[mine])).astype(BF16)
        h_ref[1] = jax.nn.gelu(mm(x, sib_ref[0, mine])).astype(BF16)
        total = mm(h_ref[0], down_ref[mine], ((1,), (1,))) + mm(h_ref[1], sib_ref[1, mine], ((1,), (1,)))
        start = 0
        for ref, i in blocks(outs, e, False):
            ref[i] = total[start:start + ref.shape[1]].astype(BF16)
            start += ref.shape[1]


def experts(chunk, blocks, sib, in_own, down_own):
    far, d1, own = blocks[0], blocks[3], blocks[5]
    per, far_rows, width = far.shape
    rows = 4 * (far_rows + own.shape[1])
    ff = sib.shape[3]
    own_shape = (per, *own.shape[1:])
    shapes = [far.shape] * 3 + [d1.shape] * 2 + [own_shape] * 4
    return list(pl.pallas_call(
        functools.partial(experts_kernel, chunk),
        out_shape=[pltpu.VMEM(shape, BF16) for shape in shapes],
        in_specs=[vmem()] * 12,
        out_specs=[vmem()] * 9,
        scratch_shapes=[pltpu.VMEM((2, rows, ff), BF16)],
        compiler_params=pltpu.CompilerParams(vmem_limit_bytes=VMEM_LIMIT),
        cost_estimate=pl.CostEstimate(
            flops=2 * per * rows * width * 2 * ff * 2, bytes_accessed=per * rows * width * 4,
            transcendentals=per * rows * 2 * ff),
        name="experts",
    )(*blocks, *(in_vmem(panel) for panel in (sib, in_own, down_own))))


def combine_kernel(tok, spans, gate_ref, emb_ref, *refs):
    own_refs, (from_a_ref, from_b_ref), piece_refs = refs[:CHUNKS], refs[CHUNKS:CHUNKS + 2], refs[CHUNKS + 2:-3]
    mine_ref, send_ref, rows_ref = refs[-3:]
    per, slots, _ = own_refs[0].shape
    for c, ref in enumerate(own_refs):
        for e in range(per):
            i = c * per + e
            done = ref[e].astype(F32) + from_a_ref[i].astype(F32) + from_b_ref[i].astype(F32)
            rows_ref[i * slots:(i + 1) * slots] = done
    for start, ref in zip(spans, piece_refs):
        for e in range(ref.shape[0]):
            rows_ref[(start + e) * slots:(start + e + 1) * slots] = ref[e].astype(F32)
    total = mm(gate_ref[...], rows_ref[...].astype(BF16), ((0,), (0,)))
    mine_ref[...] = total[0:tok] + emb_ref[...].astype(F32)
    send_ref[...] = total[tok:2 * tok].astype(BF16)


def combine(gate, embedded, own_parts, from_a, from_b, spans, pieces):
    tok, width = embedded.shape
    rows = gate.shape[0]
    return pl.pallas_call(
        functools.partial(combine_kernel, tok, spans),
        out_shape=[pltpu.VMEM((tok, width), F32), pltpu.VMEM((tok, width), BF16)],
        in_specs=[vmem()] * (4 + len(own_parts) + len(pieces)),
        out_specs=[vmem()] * 2,
        scratch_shapes=[pltpu.VMEM((rows, width), F32)],
        compiler_params=pltpu.CompilerParams(vmem_limit_bytes=VMEM_LIMIT),
        cost_estimate=pl.CostEstimate(flops=4 * tok * rows * width, bytes_accessed=rows * width * 2, transcendentals=0),
        name="combine",
    )(gate, embedded, *own_parts, from_a, from_b, *pieces)


def on_device(tubelets, embed_weight, norm_gain, routes, gate_codes, w_in, w_down):
    tok = tubelets.shape[0]
    n_exp = lax.axis_size("exp")
    half = w_in.shape[0] // 2
    cap = 3 * tok // (w_in.shape[0] * n_exp)
    position = lax.axis_index("rep")
    core = position % 2
    place = jnp.stack([lax.axis_index("exp"), core]).astype(jnp.int32)

    core_bit = 1 << CORE
    codes = jnp.concatenate([routes.T, gate_codes.T], axis=0)
    sib_codes = swapped(codes, "rep", core_bit)
    embedded, normed = embed(after(tubelets, codes), embed_weight, norm_gain)
    sib_normed = swapped(normed, "rep", core_bit)
    select, gate = route(place, codes, sib_codes, n_exp, half, cap)

    for bit in range(GROUP_BITS, lax.axis_size("rep").bit_length() - 1):
        upper = position // (1 << bit) % 2 == 1

        def gathered(panel):
            partner = swapped(panel, "rep", 1 << bit)
            return jnp.where(upper, jnp.concatenate([partner, panel], axis=2), jnp.concatenate([panel, partner], axis=2))

        w_in, w_down = gathered(w_in), gathered(w_down)

    pieces = pack(select, normed, sib_normed, n_exp, half, cap)
    per = half // CHUNKS
    split = per // 2
    a_bit, b_bit = 1 << NEAR_A, 1 << NEAR_B

    def to_a(rows):
        return swapped(rows, "rep", a_bit)

    def to_b(rows):
        return swapped(rows, "rep", b_bit)

    own = pieces[0][0]
    first = swapped(pieces[1][0], "exp", 1)
    far0 = jnp.concatenate([first[:per]] + [swapped(pieces[s][0], "exp", s) for s in range(2, n_exp)], axis=1)
    own_a, own_b = to_a(own), to_b(own)
    lent = lend(after(place, own_a, own_b), w_in, w_down)
    own_d = to_b(own_a[:per]), to_a(own_b[per:])
    far0, sib, *own_d = lax.optimization_barrier((far0, lent, *own_d))
    sib = swapped(sib, "rep", core_bit)
    late = lax.optimization_barrier((far0, *(pieces[s][1] for s in range(2, n_exp))))[1:]
    far1 = jnp.concatenate([first[per:]] + [swapped(piece, "exp", s + 2) for s, piece in enumerate(late)], axis=1)
    a0, b0 = to_a(far0), to_b(far0)
    far1 = after(far1, a0, b0)
    in_own, down_own = hold(after(place, far0), w_in, w_down)
    a0, b0 = lax.optimization_barrier((a0, b0, in_own))[:2]
    d0 = to_b(a0[:split]), to_a(b0[split:])
    a1, b1 = to_a(far1), to_b(far1)
    parts0 = experts(0, (far0, a0, b0, *d0, own, own_a, own_b, own_d[0]), sib, in_own, down_own)
    a1, b1, *parts0 = lax.optimization_barrier((a1, b1, *parts0))
    r0 = to_a(parts0[3]), to_b(parts0[4])
    d1 = to_b(a1[:split]), to_a(b1[split:])

    def reduced(parts, r):
        return (jnp.concatenate([parts[1][:split], parts[1][split:] + r[1]], axis=0),
                jnp.concatenate([parts[2][:split] + r[0], parts[2][split:]], axis=0))

    def back(part, from_a, from_b):
        done = (part.astype(F32) + from_a.astype(F32) + from_b.astype(F32)).astype(BF16)
        shifts = jnp.split(done, n_exp - 1, axis=1)
        return shifts[0], [swapped(rows, "exp", s + 2) for s, rows in enumerate(shifts[1:])]

    sums0 = reduced(parts0, r0)
    d1 = lax.optimization_barrier((*d1, *sums0))[:2]
    from_a0, from_b0 = to_a(sums0[0]), to_b(sums0[1])
    parts1 = experts(1, (far1, a1, b1, *d1, own, own_a, own_b, own_d[1]), sib, in_own, down_own)
    parts1[3], parts1[4] = lax.optimization_barrier((parts1[3], parts1[4], from_a0, from_b0))[:2]
    r1 = to_a(parts1[3]), to_b(parts1[4])
    returned0 = back(parts0[0], from_a0, from_b0)
    sums1 = reduced(parts1, r1)
    from_a1, from_b1 = to_a(sums1[0]), to_b(sums1[1])
    returned1 = back(parts1[0], from_a1, from_b1)
    own_r = to_a(after(parts0[8], from_a0, from_b0)), to_b(after(parts1[8], from_a0, from_b0))
    own_to_a = jnp.concatenate([parts0[6], parts1[6] + own_r[1]], axis=0)
    own_to_b = jnp.concatenate([parts0[7] + own_r[0], parts1[7]], axis=0)
    own_to_a, own_to_b = lax.optimization_barrier((own_to_a, own_to_b, *sums1))[:2]
    spans = [half] + [s * half + c * per for s in range(2, n_exp) for c in range(CHUNKS)]
    pieces_back = [swapped(jnp.concatenate([returned0[0], returned1[0]], axis=0), "exp", 1)]
    pieces_back += [returned[s] for s in range(n_exp - 2) for returned in (returned0[1], returned1[1])]
    mine, send = combine(
        gate, embedded, (parts0[5], parts1[5]), to_a(own_to_a), to_b(own_to_b), spans, pieces_back)
    other = swapped(send, "rep", 1 << CORE)
    return (mine + other.astype(F32)).astype(BF16)


def solution(mesh):
    return jax.shard_map(
        on_device,
        mesh=mesh,
        in_specs=(
            P(("rep", "exp"), None),
            P(),
            P(),
            P(("rep", "exp"), None),
            P(("rep", "exp"), None),
            P("exp", None, "rep"),
            P("exp", None, "rep"),
        ),
        out_specs=P(("rep", "exp"), None),
        check_vma=False,
    )
```

```python
import functools

import jax
import jax.numpy as jnp
from jax import lax
from jax.experimental import pallas as pl
from jax.experimental.pallas import tpu as pltpu
from jax.sharding import PartitionSpec as P

F32 = jnp.float32
BF16 = jnp.bfloat16
CHUNKS = 2
CORE, NEAR_A, NEAR_B = 0, 1, 2
GROUP_BITS = 3
MIB = 1024 * 1024
VMEM_LIMIT = 20 * MIB


def swapped(array, axis, distance):
    return lax.ppermute(array, axis, [(i, i ^ distance) for i in range(lax.axis_size(axis))])


def after(value, *others):
    return lax.optimization_barrier((value, *others))[0]


def early_experts(half):
    return 2 * half // 4


def mm(a, b, dims=((1,), (0,))):
    return lax.dot_general(a, b, (dims, ((), ())), preferred_element_type=F32)


def vmem():
    return pl.BlockSpec(memory_space=pltpu.VMEM)


def hbm():
    return pl.BlockSpec(memory_space=pltpu.HBM)


def in_hbm(array):
    return pltpu.with_memory_space_constraint(array, pltpu.HBM)


def in_vmem(array):
    return pltpu.with_memory_space_constraint(array, pltpu.VMEM)


def smem():
    return pl.BlockSpec(memory_space=pltpu.SMEM)


def embed_kernel(tubelets_ref, weight_ref, gain_ref, emb_ref, normed_ref, tub, weight, gain, sems):
    parts = sems.shape[0] - 2
    depth = weight_ref.shape[0] // parts
    copies = []
    for k in range(parts):
        rows = pl.ds(k * depth, depth)
        copies.append(pltpu.make_async_copy(weight_ref.at[rows], weight.at[rows], sems.at[k]))
    tub_copy = pltpu.make_async_copy(tubelets_ref, tub, sems.at[parts])
    gain_copy = pltpu.make_async_copy(gain_ref, gain, sems.at[parts + 1])
    for copy in (tub_copy, *copies, gain_copy):
        copy.start()
    tub_copy.wait()
    total = None
    for k in range(parts):
        copies[k].wait()
        rows = slice(k * depth, (k + 1) * depth)
        term = mm(tub[:, rows], weight[rows, :])
        total = term if total is None else total + term
    embedded = total.astype(BF16)
    emb_ref[...] = embedded
    floats = embedded.astype(F32)
    centred = floats - jnp.mean(floats, axis=-1, keepdims=True)
    variance = jnp.mean(centred * centred, axis=-1, keepdims=True)
    gain_copy.wait()
    normed_ref[...] = (centred * lax.rsqrt(variance + 1e-06) * gain[...]).astype(BF16)


def embed(tubelets, weight, gain):
    tok, width = tubelets.shape[0], weight.shape[1]
    parts = 6
    shape = pltpu.VMEM((tok, width), BF16)
    return pl.pallas_call(
        embed_kernel,
        out_shape=[shape, shape],
        in_specs=[hbm()] * 3,
        out_specs=[vmem()] * 2,
        scratch_shapes=[pltpu.VMEM(tubelets.shape, BF16), pltpu.VMEM(weight.shape, BF16),
                        pltpu.VMEM((1, width), F32), pltpu.SemaphoreType.DMA((parts + 2,))],
        compiler_params=pltpu.CompilerParams(vmem_limit_bytes=VMEM_LIMIT),
        cost_estimate=pl.CostEstimate(flops=2 * tok * weight.size, bytes_accessed=weight.size * 2, transcendentals=0),
        name="embed",
    )(in_hbm(tubelets), in_hbm(weight), in_hbm(gain.reshape(1, width)))


def route_kernel(n_exp, half, cap, place_ref, code_ref, sib_code_ref, select_ref, gate_ref):
    tok = code_ref.shape[1]
    both = 2 * tok
    count = n_exp * half
    slots = 2 * cap
    rows = count * slots
    codes = jnp.concatenate([code_ref[...], sib_code_ref[...]], axis=1)
    gates = 0.25 + 0.125 * codes[2:4].astype(F32)
    plane, core = place_ref[0], place_ref[1]

    row = lax.broadcasted_iota(jnp.int32, (count, both), 0)
    expert = (plane ^ (row // half)) * (2 * half) + core * half + row % half
    first = codes[0:1] == expert
    second = codes[1:2] == expert
    member = first | second
    gated = jnp.where(first, gates[0:1, :], 0.0) + jnp.where(second, gates[1:2, :], 0.0)
    earlier = lax.broadcasted_iota(jnp.int32, (both, both), 0)
    later = lax.broadcasted_iota(jnp.int32, (both, both), 1)
    before = jnp.where(((earlier // tok) == (later // tok)) & (earlier < later), 1.0, 0.0).astype(BF16)
    rank = mm(jnp.where(member, 1.0, 0.0).astype(BF16), before)
    block = jnp.where(lax.broadcasted_iota(jnp.int32, (count, both), 1) >= tok, float(cap), 0.0)
    pos = jnp.where(member, rank + block, -1.0).astype(BF16)
    spread = jnp.where(
        lax.broadcasted_iota(jnp.int32, (rows, count), 0) // slots
        == lax.broadcasted_iota(jnp.int32, (rows, count), 1), 1.0, 0.0).astype(BF16)
    slot = (lax.broadcasted_iota(jnp.int32, (rows, both), 0) % slots).astype(F32)
    chosen = mm(spread, pos) == slot
    select_ref[...] = jnp.where(chosen, 1.0, 0.0).astype(BF16)
    gate_ref[...] = jnp.where(chosen, mm(spread, gated.astype(BF16)), 0.0).astype(BF16)


def route(place, codes, sib_codes, n_exp, half, cap):
    both = 2 * codes.shape[1]
    rows = n_exp * half * 2 * cap
    shape = jax.ShapeDtypeStruct((rows, both), BF16)
    return pl.pallas_call(
        functools.partial(route_kernel, n_exp, half, cap),
        out_shape=[shape, shape],
        in_specs=[smem()] + [vmem()] * 2,
        out_specs=[vmem()] * 2,
        compiler_params=pltpu.CompilerParams(vmem_limit_bytes=VMEM_LIMIT),
        cost_estimate=pl.CostEstimate(flops=2 * rows * both * 64, bytes_accessed=rows * both * 4, transcendentals=0),
        name="route",
    )(place, codes, sib_codes)


def pack_kernel(spans, select_ref, normed_ref, sib_ref, *piece_refs):
    buffer = mm(select_ref[...], jnp.concatenate([normed_ref[...], sib_ref[...]], axis=0))
    slots = piece_refs[0].shape[1]
    for (start, count), ref in zip(spans, piece_refs):
        for e in range(count):
            ref[e] = buffer[(start + e) * slots:(start + e + 1) * slots].astype(BF16)


def pack(select, normed, sib_normed, n_exp, half, cap):
    width = normed.shape[1]
    rows = select.shape[0]
    cut = early_experts(half)
    spans = []
    for s in range(n_exp):
        spans += [(s * half, half)] if s < 2 else [(s * half, cut), (s * half + cut, half - cut)]
    pieces = list(pl.pallas_call(
        functools.partial(pack_kernel, spans),
        out_shape=[pltpu.VMEM((count, 2 * cap, width), BF16) for _, count in spans],
        in_specs=[vmem()] * 3,
        out_specs=[vmem()] * len(spans),
        compiler_params=pltpu.CompilerParams(vmem_limit_bytes=VMEM_LIMIT),
        cost_estimate=pl.CostEstimate(
            flops=2 * select.size * width, bytes_accessed=rows * width * 4, transcendentals=0),
        name="pack",
    )(select, normed, sib_normed))
    return [[pieces.pop(0)] if s < 2 else [pieces.pop(0) for _ in range(CHUNKS)] for s in range(n_exp)]


def lend_kernel(place_ref, in_ref, down_ref, out_ref, sems):
    count = out_ref.shape[1]
    start = (1 - place_ref[1]) * count
    copies = []
    for e in range(count):
        for which, source in enumerate((in_ref, down_ref)):
            copies.append(pltpu.make_async_copy(source.at[start + e], out_ref.at[which, e], sems.at[which, e]))
            copies[-1].start()
    for copy in copies:
        copy.wait()


def lend(place, w_in, w_down):
    shape = (2, w_in.shape[0] // 2, *w_in.shape[1:])
    return pl.pallas_call(
        lend_kernel,
        out_shape=pltpu.VMEM(shape, BF16),
        in_specs=[smem(), hbm(), hbm()],
        out_specs=vmem(),
        scratch_shapes=[pltpu.SemaphoreType.DMA(shape[:2])],
        compiler_params=pltpu.CompilerParams(vmem_limit_bytes=VMEM_LIMIT),
        cost_estimate=pl.CostEstimate(flops=0, bytes_accessed=w_in.size * 4, transcendentals=0),
        name="lend",
    )(place, in_hbm(w_in), in_hbm(w_down))


def hold_kernel(place_ref, in_ref, down_ref, in_out, down_out, sems):
    count = in_out.shape[0]
    copies = []
    for e in range(count):
        index = place_ref[1] * count + e
        for which, (source, target) in enumerate(((in_ref, in_out), (down_ref, down_out))):
            copies.append(pltpu.make_async_copy(source.at[index], target.at[e], sems.at[which, e]))
            copies[-1].start()
    for copy in copies:
        copy.wait()


def hold(place, w_in, w_down):
    shape = pltpu.VMEM((w_in.shape[0] // 2, *w_in.shape[1:]), BF16)
    return pl.pallas_call(
        hold_kernel,
        out_shape=[shape, shape],
        in_specs=[smem(), hbm(), hbm()],
        out_specs=[vmem()] * 2,
        scratch_shapes=[pltpu.SemaphoreType.DMA((2, w_in.shape[0] // 2))],
        compiler_params=pltpu.CompilerParams(vmem_limit_bytes=VMEM_LIMIT),
        cost_estimate=pl.CostEstimate(flops=0, bytes_accessed=w_in.size * 4, transcendentals=0),
        name="hold",
    )(place, in_hbm(w_in), in_hbm(w_down))


def experts_kernel(first, *refs):
    rows_refs, (sib_ref, in_ref, down_ref), outs, h_ref = refs[:10], refs[10:13], refs[13:22], refs[22]
    far, far_a, far_b, d1, d2, own, own_a, own_b, own_d1, own_d2 = rows_refs
    per, split = far.shape[0], own_d1.shape[0]
    for e in range(per):
        mine = first + e
        own_d = own_d1[mine] if mine < split else own_d2[mine - split]
        x = jnp.concatenate(
            [ref[e] for ref in (far, far_a, far_b, d1, d2)] + [ref[mine] for ref in (own, own_a, own_b)] + [own_d], axis=0)
        h_ref[0] = jax.nn.gelu(mm(x, in_ref[mine])).astype(BF16)
        h_ref[1] = jax.nn.gelu(mm(x, sib_ref[0, mine])).astype(BF16)
        total = mm(h_ref[0], down_ref[mine], ((1,), (1,))) + mm(h_ref[1], sib_ref[1, mine], ((1,), (1,)))
        start = 0
        for ref in outs:
            ref[e] = total[start:start + ref.shape[1]].astype(BF16)
            start += ref.shape[1]


def experts(first, blocks, sib, in_own, down_own):
    far, own = blocks[0], blocks[5]
    per, far_rows, width = far.shape
    rows = 4 * (far_rows + own.shape[1])
    ff = sib.shape[3]
    shapes = [block.shape for block in blocks[:5]] + [(per, *own.shape[1:])] * 4
    return list(pl.pallas_call(
        functools.partial(experts_kernel, first),
        out_shape=[pltpu.VMEM(shape, BF16) for shape in shapes],
        in_specs=[vmem()] * 13,
        out_specs=[vmem()] * 9,
        scratch_shapes=[pltpu.VMEM((2, rows, ff), BF16)],
        compiler_params=pltpu.CompilerParams(vmem_limit_bytes=VMEM_LIMIT),
        cost_estimate=pl.CostEstimate(
            flops=2 * per * rows * width * 2 * ff * 2, bytes_accessed=per * rows * width * 4,
            transcendentals=per * rows * 2 * ff),
        name="experts",
    )(*blocks, *(in_vmem(panel) for panel in (sib, in_own, down_own))))


def combine_kernel(tok, spans, gate_ref, emb_ref, *refs):
    own_refs, (from_a_ref, from_b_ref), piece_refs = refs[:CHUNKS], refs[CHUNKS:CHUNKS + 2], refs[CHUNKS + 2:-3]
    mine_ref, send_ref, rows_ref = refs[-3:]
    slots = own_refs[0].shape[1]
    for c, ref in enumerate(own_refs):
        for e in range(ref.shape[0]):
            i = c * own_refs[0].shape[0] + e
            done = ref[e].astype(F32) + from_a_ref[i].astype(F32) + from_b_ref[i].astype(F32)
            rows_ref[i * slots:(i + 1) * slots] = done
    for start, ref in zip(spans, piece_refs):
        for e in range(ref.shape[0]):
            rows_ref[(start + e) * slots:(start + e + 1) * slots] = ref[e].astype(F32)
    total = mm(gate_ref[...], rows_ref[...].astype(BF16), ((0,), (0,)))
    mine_ref[...] = total[0:tok] + emb_ref[...].astype(F32)
    send_ref[...] = total[tok:2 * tok].astype(BF16)


def combine(gate, embedded, own_parts, from_a, from_b, spans, pieces):
    tok, width = embedded.shape
    rows = gate.shape[0]
    return pl.pallas_call(
        functools.partial(combine_kernel, tok, spans),
        out_shape=[pltpu.VMEM((tok, width), F32), pltpu.VMEM((tok, width), BF16)],
        in_specs=[vmem()] * (4 + len(own_parts) + len(pieces)),
        out_specs=[vmem()] * 2,
        scratch_shapes=[pltpu.VMEM((rows, width), F32)],
        compiler_params=pltpu.CompilerParams(vmem_limit_bytes=VMEM_LIMIT),
        cost_estimate=pl.CostEstimate(flops=4 * tok * rows * width, bytes_accessed=rows * width * 2, transcendentals=0),
        name="combine",
    )(gate, embedded, *own_parts, from_a, from_b, *pieces)


def on_device(tubelets, embed_weight, norm_gain, routes, gate_codes, w_in, w_down):
    tok = tubelets.shape[0]
    n_exp = lax.axis_size("exp")
    half = w_in.shape[0] // 2
    cap = 3 * tok // (w_in.shape[0] * n_exp)
    position = lax.axis_index("rep")
    core = position % 2
    place = jnp.stack([lax.axis_index("exp"), core]).astype(jnp.int32)

    core_bit = 1 << CORE
    codes = jnp.concatenate([routes.T, gate_codes.T], axis=0)
    sib_codes = swapped(codes, "rep", core_bit)
    embedded, normed = embed(after(tubelets, codes), embed_weight, norm_gain)
    sib_normed = swapped(normed, "rep", core_bit)
    select, gate = route(place, codes, sib_codes, n_exp, half, cap)

    for bit in range(GROUP_BITS, lax.axis_size("rep").bit_length() - 1):
        upper = position // (1 << bit) % 2 == 1

        def gathered(panel):
            partner = swapped(panel, "rep", 1 << bit)
            return jnp.where(upper, jnp.concatenate([partner, panel], axis=2), jnp.concatenate([panel, partner], axis=2))

        w_in, w_down = gathered(w_in), gathered(w_down)

    pieces = pack(select, normed, sib_normed, n_exp, half, cap)
    cut, split = early_experts(half), half // 2
    a_bit, b_bit = 1 << NEAR_A, 1 << NEAR_B

    def to_a(rows):
        return swapped(rows, "rep", a_bit)

    def to_b(rows):
        return swapped(rows, "rep", b_bit)

    own = pieces[0][0]
    first = swapped(pieces[1][0], "exp", 1)
    far0 = jnp.concatenate([first[:cut]] + [swapped(pieces[s][0], "exp", s) for s in range(2, n_exp)], axis=1)
    own_a, own_b = to_a(own), to_b(own)
    lent = lend(after(place, own_a, own_b), w_in, w_down)
    own_d = to_b(own_a[:split]), to_a(own_b[split:])
    far0, sib, *own_d = lax.optimization_barrier((far0, lent, *own_d))
    sib = swapped(sib, "rep", core_bit)
    shifts1 = list(range(n_exp - 1, 1, -1))
    late = lax.optimization_barrier((far0, *(pieces[s][1] for s in shifts1)))[1:]
    far1 = jnp.concatenate([first[cut:]] + [swapped(piece, "exp", s) for s, piece in zip(shifts1, late)], axis=1)
    a0, b0 = to_a(far0), to_b(far0)
    far1 = after(far1, a0, b0)
    in_own, down_own = hold(after(place, far0), w_in, w_down)
    a0, b0 = lax.optimization_barrier((a0, b0, in_own))[:2]
    turn = far0.shape[1] // 16 * 8
    d0 = to_b(a0[:, :turn]), to_a(b0[:, turn:])
    a1, b1 = to_a(far1), to_b(far1)
    parts0 = experts(0, (far0, a0, b0, *d0, own, own_a, own_b, *own_d), sib, in_own, down_own)
    a1, b1, *parts0 = lax.optimization_barrier((a1, b1, *parts0))
    r0 = to_a(parts0[3]), to_b(parts0[4])
    d1 = to_b(a1[:, :turn]), to_a(b1[:, turn:])

    def reduced(parts, r):
        return (jnp.concatenate([parts[1][:, :turn], parts[1][:, turn:] + r[1]], axis=1),
                jnp.concatenate([parts[2][:, :turn] + r[0], parts[2][:, turn:]], axis=1))

    def back(part, from_a, from_b, order):
        done = (part.astype(F32) + from_a.astype(F32) + from_b.astype(F32)).astype(BF16)
        shifts = jnp.split(done, n_exp - 1, axis=1)
        return shifts[0], {s: swapped(rows, "exp", s) for s, rows in zip(order, shifts[1:])}

    sums0 = reduced(parts0, r0)
    d1 = lax.optimization_barrier((*d1, *sums0))[:2]
    from_a0, from_b0 = to_a(sums0[0]), to_b(sums0[1])
    parts1 = experts(cut, (far1, a1, b1, *d1, own, own_a, own_b, *own_d), sib, in_own, down_own)
    parts1[3], parts1[4] = lax.optimization_barrier((parts1[3], parts1[4], from_a0, from_b0))[:2]
    r1 = to_a(parts1[3]), to_b(parts1[4])
    returned0 = back(parts0[0], from_a0, from_b0, range(2, n_exp))
    sums1 = reduced(parts1, r1)
    from_a1, from_b1 = to_a(sums1[0]), to_b(sums1[1])
    returned1 = back(parts1[0], from_a1, from_b1, shifts1)
    across = jnp.concatenate([parts0[8], parts1[8]], axis=0)
    across = after(across, from_a0, from_b0)
    own_r = to_a(across[:split]), to_b(across[split:])
    own_to_a = jnp.concatenate([parts0[6], parts1[6]], axis=0)
    own_to_b = jnp.concatenate([parts0[7], parts1[7]], axis=0)
    own_to_a = jnp.concatenate([own_to_a[:split], own_to_a[split:] + own_r[1]], axis=0)
    own_to_b = jnp.concatenate([own_to_b[:split] + own_r[0], own_to_b[split:]], axis=0)
    own_to_a, own_to_b = lax.optimization_barrier((own_to_a, own_to_b, *sums1))[:2]
    spans = [half] + [s * half + start for s in range(2, n_exp) for start in (0, cut)]
    pieces_back = [swapped(jnp.concatenate([returned0[0], returned1[0]], axis=0), "exp", 1)]
    pieces_back += [returned[s] for s in range(2, n_exp) for returned in (returned0[1], returned1[1])]
    mine, send = combine(
        gate, embedded, (parts0[5], parts1[5]), to_a(own_to_a), to_b(own_to_b), spans, pieces_back)
    other = swapped(send, "rep", 1 << CORE)
    return (mine + other.astype(F32)).astype(BF16)


def solution(mesh):
    return jax.shard_map(
        on_device,
        mesh=mesh,
        in_specs=(
            P(("rep", "exp"), None),
            P(),
            P(),
            P(("rep", "exp"), None),
            P(("rep", "exp"), None),
            P("exp", None, "rep"),
            P("exp", None, "rep"),
        ),
        out_specs=P(("rep", "exp"), None),
        check_vma=False,
    )
```

```python
import functools

import jax
import jax.numpy as jnp
from jax import lax
from jax.experimental import pallas as pl
from jax.experimental.pallas import tpu as pltpu
from jax.sharding import PartitionSpec as P

F32 = jnp.float32
BF16 = jnp.bfloat16
CHUNKS = 2
CORE, NEAR_A, NEAR_B = 0, 1, 2
GROUP_BITS = 3
MIB = 1024 * 1024
VMEM_LIMIT = 20 * MIB


def swapped(array, axis, distance):
    return lax.ppermute(array, axis, [(i, i ^ distance) for i in range(lax.axis_size(axis))])


def after(value, *others):
    return lax.optimization_barrier((value, *others))[0]


def early_experts(half):
    return 2 * half // 4


def mm(a, b, dims=((1,), (0,))):
    return lax.dot_general(a, b, (dims, ((), ())), preferred_element_type=F32)


def vmem():
    return pl.BlockSpec(memory_space=pltpu.VMEM)


def hbm():
    return pl.BlockSpec(memory_space=pltpu.HBM)


def in_hbm(array):
    return pltpu.with_memory_space_constraint(array, pltpu.HBM)


def in_vmem(array):
    return pltpu.with_memory_space_constraint(array, pltpu.VMEM)


def smem():
    return pl.BlockSpec(memory_space=pltpu.SMEM)


def embed_kernel(tubelets_ref, weight_ref, gain_ref, route_ref, code_ref,
                 emb_ref, normed_ref, route_out, code_out, tub, weight, gain, sems):
    parts = sems.shape[0] - 4
    depth = weight_ref.shape[0] // parts
    copies = []
    for k in range(parts):
        rows = pl.ds(k * depth, depth)
        copies.append(pltpu.make_async_copy(weight_ref.at[rows], weight.at[rows], sems.at[k]))
    tub_copy = pltpu.make_async_copy(tubelets_ref, tub, sems.at[parts])
    gain_copy = pltpu.make_async_copy(gain_ref, gain, sems.at[parts + 1])
    small = [gain_copy, pltpu.make_async_copy(route_ref, route_out, sems.at[parts + 2]),
             pltpu.make_async_copy(code_ref, code_out, sems.at[parts + 3])]
    for copy in (tub_copy, *copies, *small):
        copy.start()
    tub_copy.wait()
    total = None
    for k in range(parts):
        copies[k].wait()
        rows = slice(k * depth, (k + 1) * depth)
        term = mm(tub[:, rows], weight[rows, :])
        total = term if total is None else total + term
    embedded = total.astype(BF16)
    emb_ref[...] = embedded
    floats = embedded.astype(F32)
    centred = floats - jnp.mean(floats, axis=-1, keepdims=True)
    variance = jnp.mean(centred * centred, axis=-1, keepdims=True)
    for copy in small:
        copy.wait()
    normed_ref[...] = (centred * lax.rsqrt(variance + 1e-06) * gain[...]).astype(BF16)


def embed(tubelets, weight, gain, routes, codes):
    tok, width = tubelets.shape[0], weight.shape[1]
    parts = 6
    shape = pltpu.VMEM((tok, width), BF16)
    return pl.pallas_call(
        embed_kernel,
        out_shape=[shape, shape, pltpu.VMEM(routes.shape, routes.dtype), pltpu.VMEM(codes.shape, codes.dtype)],
        in_specs=[hbm()] * 5,
        out_specs=[vmem()] * 4,
        scratch_shapes=[pltpu.VMEM(tubelets.shape, BF16), pltpu.VMEM(weight.shape, BF16),
                        pltpu.VMEM((1, width), F32), pltpu.SemaphoreType.DMA((parts + 4,))],
        compiler_params=pltpu.CompilerParams(vmem_limit_bytes=VMEM_LIMIT),
        cost_estimate=pl.CostEstimate(flops=2 * tok * weight.size, bytes_accessed=weight.size * 2, transcendentals=0),
        name="embed",
    )(in_hbm(tubelets), in_hbm(weight), in_hbm(gain.reshape(1, width)), in_hbm(routes), in_hbm(codes))


def route_kernel(n_exp, half, cap, place_ref, route_ref, sib_route_ref, code_ref, sib_code_ref, select_ref, gate_ref):
    tok = code_ref.shape[1]
    both = 2 * tok
    count = n_exp * half
    slots = 2 * cap
    rows = count * slots
    routes = jnp.concatenate([route_ref[...], sib_route_ref[...]], axis=1)
    codes = jnp.concatenate([code_ref[...], sib_code_ref[...]], axis=1)
    gates = 0.25 + 0.125 * codes.astype(F32)
    plane, core = place_ref[0], place_ref[1]

    row = lax.broadcasted_iota(jnp.int32, (count, both), 0)
    expert = (plane ^ (row // half)) * (2 * half) + core * half + row % half
    first = routes[0:1] == expert
    second = routes[1:2] == expert
    member = first | second
    gated = jnp.where(first, gates[0:1, :], 0.0) + jnp.where(second, gates[1:2, :], 0.0)
    earlier = lax.broadcasted_iota(jnp.int32, (both, both), 0)
    later = lax.broadcasted_iota(jnp.int32, (both, both), 1)
    before = jnp.where(((earlier // tok) == (later // tok)) & (earlier < later), 1.0, 0.0).astype(BF16)
    rank = mm(jnp.where(member, 1.0, 0.0).astype(BF16), before)
    block = jnp.where(lax.broadcasted_iota(jnp.int32, (count, both), 1) >= tok, float(cap), 0.0)
    pos = jnp.where(member, rank + block, -1.0).astype(BF16)
    spread = jnp.where(
        lax.broadcasted_iota(jnp.int32, (rows, count), 0) // slots
        == lax.broadcasted_iota(jnp.int32, (rows, count), 1), 1.0, 0.0).astype(BF16)
    slot = (lax.broadcasted_iota(jnp.int32, (rows, both), 0) % slots).astype(F32)
    chosen = mm(spread, pos) == slot
    select_ref[...] = jnp.where(chosen, 1.0, 0.0).astype(BF16)
    gate_ref[...] = jnp.where(chosen, mm(spread, gated.astype(BF16)), 0.0).astype(BF16)


def route(place, routes, sib_routes, codes, sib_codes, n_exp, half, cap):
    both = 2 * codes.shape[1]
    rows = n_exp * half * 2 * cap
    shape = jax.ShapeDtypeStruct((rows, both), BF16)
    return pl.pallas_call(
        functools.partial(route_kernel, n_exp, half, cap),
        out_shape=[shape, shape],
        in_specs=[smem()] + [vmem()] * 4,
        out_specs=[vmem()] * 2,
        compiler_params=pltpu.CompilerParams(vmem_limit_bytes=VMEM_LIMIT),
        cost_estimate=pl.CostEstimate(flops=2 * rows * both * 64, bytes_accessed=rows * both * 4, transcendentals=0),
        name="route",
    )(place, routes, sib_routes, codes, sib_codes)


def pack_kernel(spans, select_ref, normed_ref, sib_ref, *piece_refs):
    buffer = mm(select_ref[...], jnp.concatenate([normed_ref[...], sib_ref[...]], axis=0))
    slots = piece_refs[0].shape[1]
    for (start, count), ref in zip(spans, piece_refs):
        for e in range(count):
            ref[e] = buffer[(start + e) * slots:(start + e + 1) * slots].astype(BF16)


def pack(select, normed, sib_normed, n_exp, half, cap):
    width = normed.shape[1]
    rows = select.shape[0]
    cut = early_experts(half)
    spans = []
    for s in range(n_exp):
        spans += [(s * half, half)] if s < 2 else [(s * half, cut), (s * half + cut, half - cut)]
    pieces = list(pl.pallas_call(
        functools.partial(pack_kernel, spans),
        out_shape=[pltpu.VMEM((count, 2 * cap, width), BF16) for _, count in spans],
        in_specs=[vmem()] * 3,
        out_specs=[vmem()] * len(spans),
        compiler_params=pltpu.CompilerParams(vmem_limit_bytes=VMEM_LIMIT),
        cost_estimate=pl.CostEstimate(
            flops=2 * select.size * width, bytes_accessed=rows * width * 4, transcendentals=0),
        name="pack",
    )(select, normed, sib_normed))
    return [[pieces.pop(0)] if s < 2 else [pieces.pop(0) for _ in range(CHUNKS)] for s in range(n_exp)]


def lend_kernel(place_ref, in_ref, down_ref, out_ref, sems):
    count = out_ref.shape[1]
    start = (1 - place_ref[1]) * count
    copies = []
    for e in range(count):
        for which, source in enumerate((in_ref, down_ref)):
            copies.append(pltpu.make_async_copy(source.at[start + e], out_ref.at[which, e], sems.at[which, e]))
            copies[-1].start()
    for copy in copies:
        copy.wait()


def lend(place, w_in, w_down):
    shape = (2, w_in.shape[0] // 2, *w_in.shape[1:])
    return pl.pallas_call(
        lend_kernel,
        out_shape=pltpu.VMEM(shape, BF16),
        in_specs=[smem(), hbm(), hbm()],
        out_specs=vmem(),
        scratch_shapes=[pltpu.SemaphoreType.DMA(shape[:2])],
        compiler_params=pltpu.CompilerParams(vmem_limit_bytes=VMEM_LIMIT),
        cost_estimate=pl.CostEstimate(flops=0, bytes_accessed=w_in.size * 4, transcendentals=0),
        name="lend",
    )(place, in_hbm(w_in), in_hbm(w_down))


def hold_kernel(place_ref, in_ref, down_ref, in_out, down_out, sems):
    count = in_out.shape[0]
    copies = []
    for e in range(count):
        index = place_ref[1] * count + e
        for which, (source, target) in enumerate(((in_ref, in_out), (down_ref, down_out))):
            copies.append(pltpu.make_async_copy(source.at[index], target.at[e], sems.at[which, e]))
            copies[-1].start()
    for copy in copies:
        copy.wait()


def hold(place, w_in, w_down):
    shape = pltpu.VMEM((w_in.shape[0] // 2, *w_in.shape[1:]), BF16)
    return pl.pallas_call(
        hold_kernel,
        out_shape=[shape, shape],
        in_specs=[smem(), hbm(), hbm()],
        out_specs=[vmem()] * 2,
        scratch_shapes=[pltpu.SemaphoreType.DMA((2, w_in.shape[0] // 2))],
        compiler_params=pltpu.CompilerParams(vmem_limit_bytes=VMEM_LIMIT),
        cost_estimate=pl.CostEstimate(flops=0, bytes_accessed=w_in.size * 4, transcendentals=0),
        name="hold",
    )(place, in_hbm(w_in), in_hbm(w_down))


def experts_kernel(first, *refs):
    rows_refs, (sib_ref, in_ref, down_ref), outs, h_ref = refs[:10], refs[10:13], refs[13:22], refs[22]
    far, far_a, far_b, d1, d2, own, own_a, own_b, own_d1, own_d2 = rows_refs
    per, split = far.shape[0], own_d1.shape[0]
    for e in range(per):
        mine = first + e
        own_d = own_d1[mine] if mine < split else own_d2[mine - split]
        x = jnp.concatenate(
            [ref[e] for ref in (far, far_a, far_b, d1, d2)] + [ref[mine] for ref in (own, own_a, own_b)] + [own_d], axis=0)
        h_ref[0] = jax.nn.gelu(mm(x, in_ref[mine])).astype(BF16)
        h_ref[1] = jax.nn.gelu(mm(x, sib_ref[0, mine])).astype(BF16)
        total = mm(h_ref[0], down_ref[mine], ((1,), (1,))) + mm(h_ref[1], sib_ref[1, mine], ((1,), (1,)))
        start = 0
        for ref in outs:
            ref[e] = total[start:start + ref.shape[1]].astype(BF16)
            start += ref.shape[1]


def experts(first, blocks, sib, in_own, down_own):
    far, own = blocks[0], blocks[5]
    per, far_rows, width = far.shape
    rows = 4 * (far_rows + own.shape[1])
    ff = sib.shape[3]
    shapes = [block.shape for block in blocks[:5]] + [(per, *own.shape[1:])] * 4
    return list(pl.pallas_call(
        functools.partial(experts_kernel, first),
        out_shape=[pltpu.VMEM(shape, BF16) for shape in shapes],
        in_specs=[vmem()] * 13,
        out_specs=[vmem()] * 9,
        scratch_shapes=[pltpu.VMEM((2, rows, ff), BF16)],
        compiler_params=pltpu.CompilerParams(vmem_limit_bytes=VMEM_LIMIT),
        cost_estimate=pl.CostEstimate(
            flops=2 * per * rows * width * 2 * ff * 2, bytes_accessed=per * rows * width * 4,
            transcendentals=per * rows * 2 * ff),
        name="experts",
    )(*blocks, *(in_vmem(panel) for panel in (sib, in_own, down_own))))


def combine_kernel(tok, spans, gate_ref, emb_ref, *refs):
    own_refs, (from_a_ref, from_b_ref), piece_refs = refs[:CHUNKS], refs[CHUNKS:CHUNKS + 2], refs[CHUNKS + 2:-3]
    mine_ref, send_ref, rows_ref = refs[-3:]
    slots = own_refs[0].shape[1]
    for c, ref in enumerate(own_refs):
        for e in range(ref.shape[0]):
            i = c * own_refs[0].shape[0] + e
            done = ref[e].astype(F32) + from_a_ref[i].astype(F32) + from_b_ref[i].astype(F32)
            rows_ref[i * slots:(i + 1) * slots] = done
    for start, ref in zip(spans, piece_refs):
        for e in range(ref.shape[0]):
            rows_ref[(start + e) * slots:(start + e + 1) * slots] = ref[e].astype(F32)
    total = mm(gate_ref[...], rows_ref[...].astype(BF16), ((0,), (0,)))
    mine_ref[...] = total[0:tok] + emb_ref[...].astype(F32)
    send_ref[...] = total[tok:2 * tok].astype(BF16)


def combine(gate, embedded, own_parts, from_a, from_b, spans, pieces):
    tok, width = embedded.shape
    rows = gate.shape[0]
    return pl.pallas_call(
        functools.partial(combine_kernel, tok, spans),
        out_shape=[pltpu.VMEM((tok, width), F32), pltpu.VMEM((tok, width), BF16)],
        in_specs=[vmem()] * (4 + len(own_parts) + len(pieces)),
        out_specs=[vmem()] * 2,
        scratch_shapes=[pltpu.VMEM((rows, width), F32)],
        compiler_params=pltpu.CompilerParams(vmem_limit_bytes=VMEM_LIMIT),
        cost_estimate=pl.CostEstimate(flops=4 * tok * rows * width, bytes_accessed=rows * width * 2, transcendentals=0),
        name="combine",
    )(gate, embedded, *own_parts, from_a, from_b, *pieces)


def on_device(tubelets, embed_weight, norm_gain, routes, gate_codes, w_in, w_down):
    tok = tubelets.shape[0]
    n_exp = lax.axis_size("exp")
    half = w_in.shape[0] // 2
    cap = 3 * tok // (w_in.shape[0] * n_exp)
    position = lax.axis_index("rep")
    core = position % 2
    place = jnp.stack([lax.axis_index("exp"), core]).astype(jnp.int32)

    core_bit = 1 << CORE
    routes, codes = routes.T, gate_codes.T
    sib_routes, sib_codes = swapped(routes, "rep", core_bit), swapped(codes, "rep", core_bit)
    embedded, normed, routes, codes = embed(tubelets, embed_weight, norm_gain, routes, codes)
    sib_normed = swapped(normed, "rep", core_bit)
    select, gate = route(place, routes, sib_routes, codes, sib_codes, n_exp, half, cap)

    for bit in range(GROUP_BITS, lax.axis_size("rep").bit_length() - 1):
        upper = position // (1 << bit) % 2 == 1

        def gathered(panel):
            partner = swapped(panel, "rep", 1 << bit)
            return jnp.where(upper, jnp.concatenate([partner, panel], axis=2), jnp.concatenate([panel, partner], axis=2))

        w_in, w_down = gathered(w_in), gathered(w_down)

    pieces = pack(select, normed, sib_normed, n_exp, half, cap)
    cut, split = early_experts(half), half // 2
    a_bit, b_bit = 1 << NEAR_A, 1 << NEAR_B

    def to_a(rows):
        return swapped(rows, "rep", a_bit)

    def to_b(rows):
        return swapped(rows, "rep", b_bit)

    own = pieces[0][0]
    first = swapped(pieces[1][0], "exp", 1)
    far0 = jnp.concatenate([first[:cut]] + [swapped(pieces[s][0], "exp", s) for s in range(2, n_exp)], axis=1)
    own_a, own_b = to_a(own), to_b(own)
    lent = lend(after(place, own_a, own_b), w_in, w_down)
    own_d = to_b(own_a[:split]), to_a(own_b[split:])
    far0, sib, *own_d = lax.optimization_barrier((far0, lent, *own_d))
    sib = swapped(sib, "rep", core_bit)
    shifts1 = list(range(n_exp - 1, 1, -1))
    late = lax.optimization_barrier((far0, *(pieces[s][1] for s in shifts1)))[1:]
    far1 = jnp.concatenate([first[cut:]] + [swapped(piece, "exp", s) for s, piece in zip(shifts1, late)], axis=1)
    a0, b0 = to_a(far0), to_b(far0)
    far1 = after(far1, a0, b0)
    in_own, down_own = hold(after(place, far0), w_in, w_down)
    a0, b0 = lax.optimization_barrier((a0, b0, in_own))[:2]
    turn = far0.shape[1] // 16 * 8
    d0 = to_b(a0[:, :turn]), to_a(b0[:, turn:])
    a1, b1 = to_a(far1), to_b(far1)
    parts0 = experts(0, (far0, a0, b0, *d0, own, own_a, own_b, *own_d), sib, in_own, down_own)
    a1, b1, *parts0 = lax.optimization_barrier((a1, b1, *parts0))
    r0 = to_a(parts0[3]), to_b(parts0[4])
    d1 = to_b(a1[:, :turn]), to_a(b1[:, turn:])

    def reduced(parts, r):
        return (jnp.concatenate([parts[1][:, :turn], parts[1][:, turn:] + r[1]], axis=1),
                jnp.concatenate([parts[2][:, :turn] + r[0], parts[2][:, turn:]], axis=1))

    def back(part, from_a, from_b, order):
        done = (part.astype(F32) + from_a.astype(F32) + from_b.astype(F32)).astype(BF16)
        shifts = jnp.split(done, n_exp - 1, axis=1)
        return shifts[0], {s: swapped(rows, "exp", s) for s, rows in zip(order, shifts[1:])}

    sums0 = reduced(parts0, r0)
    d1 = lax.optimization_barrier((*d1, *sums0))[:2]
    from_a0, from_b0 = to_a(sums0[0]), to_b(sums0[1])
    parts1 = experts(cut, (far1, a1, b1, *d1, own, own_a, own_b, *own_d), sib, in_own, down_own)
    parts1[3], parts1[4] = lax.optimization_barrier((parts1[3], parts1[4], from_b0))[:2]
    r1 = to_a(parts1[3]), to_b(parts1[4])
    returned0 = back(parts0[0], from_a0, from_b0, range(2, n_exp))
    sums1 = reduced(parts1, r1)
    from_a1, from_b1 = to_a(sums1[0]), to_b(sums1[1])
    returned1 = back(parts1[0], from_a1, from_b1, shifts1)
    across = jnp.concatenate([parts0[8], parts1[8]], axis=0)
    across = after(across, from_a0, from_b0)
    own_r = to_a(across[:split]), to_b(across[split:])
    own_to_a = jnp.concatenate([parts0[6], parts1[6]], axis=0)
    own_to_b = jnp.concatenate([parts0[7], parts1[7]], axis=0)
    own_to_a = jnp.concatenate([own_to_a[:split], own_to_a[split:] + own_r[1]], axis=0)
    own_to_b = jnp.concatenate([own_to_b[:split] + own_r[0], own_to_b[split:]], axis=0)
    own_to_a, own_to_b = lax.optimization_barrier((own_to_a, own_to_b, *sums1))[:2]
    spans = [half] + [s * half + start for s in range(2, n_exp) for start in (0, cut)]
    pieces_back = [swapped(jnp.concatenate([returned0[0], returned1[0]], axis=0), "exp", 1)]
    pieces_back += [returned[s] for s in range(2, n_exp) for returned in (returned0[1], returned1[1])]
    mine, send = combine(
        gate, embedded, (parts0[5], parts1[5]), to_a(own_to_a), to_b(own_to_b), spans, pieces_back)
    other = swapped(send, "rep", 1 << CORE)
    return (mine + other.astype(F32)).astype(BF16)


def solution(mesh):
    return jax.shard_map(
        on_device,
        mesh=mesh,
        in_specs=(
            P(("rep", "exp"), None),
            P(),
            P(),
            P(("rep", "exp"), None),
            P(("rep", "exp"), None),
            P("exp", None, "rep"),
            P("exp", None, "rep"),
        ),
        out_specs=P(("rep", "exp"), None),
        check_vma=False,
    )
```

```python
import functools

import jax
import jax.numpy as jnp
from jax import lax
from jax.experimental import pallas as pl
from jax.experimental.pallas import tpu as pltpu
from jax.sharding import PartitionSpec as P

F32 = jnp.float32
BF16 = jnp.bfloat16
CHUNKS = 2
CORE, NEAR_A, NEAR_B = 0, 1, 2
GROUP_BITS = 3
MIB = 1024 * 1024
VMEM_LIMIT = 20 * MIB


def swapped(array, axis, distance):
    return lax.ppermute(array, axis, [(i, i ^ distance) for i in range(lax.axis_size(axis))])


def after(value, *others):
    return lax.optimization_barrier((value, *others))[0]


def early_experts(half):
    return 2 * half // 4


def mm(a, b, dims=((1,), (0,))):
    return lax.dot_general(a, b, (dims, ((), ())), preferred_element_type=F32)


def vmem():
    return pl.BlockSpec(memory_space=pltpu.VMEM)


def hbm():
    return pl.BlockSpec(memory_space=pltpu.HBM)


def in_hbm(array):
    return pltpu.with_memory_space_constraint(array, pltpu.HBM)


def in_vmem(array):
    return pltpu.with_memory_space_constraint(array, pltpu.VMEM)


def smem():
    return pl.BlockSpec(memory_space=pltpu.SMEM)


def embed_kernel(tubelets_ref, weight_ref, gain_ref, route_ref, code_ref,
                 emb_ref, normed_ref, route_out, code_out, tub, weight, gain, sems):
    parts = sems.shape[0] - 4
    depth = weight_ref.shape[0] // parts
    copies = []
    for k in range(parts):
        rows = pl.ds(k * depth, depth)
        copies.append(pltpu.make_async_copy(weight_ref.at[rows], weight.at[rows], sems.at[k]))
    tub_copy = pltpu.make_async_copy(tubelets_ref, tub, sems.at[parts])
    gain_copy = pltpu.make_async_copy(gain_ref, gain, sems.at[parts + 1])
    small = [gain_copy, pltpu.make_async_copy(route_ref, route_out, sems.at[parts + 2]),
             pltpu.make_async_copy(code_ref, code_out, sems.at[parts + 3])]
    for copy in (tub_copy, *copies, *small):
        copy.start()
    tub_copy.wait()
    total = None
    for k in range(parts):
        copies[k].wait()
        rows = slice(k * depth, (k + 1) * depth)
        term = mm(tub[:, rows], weight[rows, :])
        total = term if total is None else total + term
    embedded = total.astype(BF16)
    emb_ref[...] = embedded
    floats = embedded.astype(F32)
    centred = floats - jnp.mean(floats, axis=-1, keepdims=True)
    variance = jnp.mean(centred * centred, axis=-1, keepdims=True)
    for copy in small:
        copy.wait()
    normed_ref[...] = (centred * lax.rsqrt(variance + 1e-06) * gain[...]).astype(BF16)


def embed(tubelets, weight, gain, routes, codes):
    tok, width = tubelets.shape[0], weight.shape[1]
    parts = 6
    shape = pltpu.VMEM((tok, width), BF16)
    return pl.pallas_call(
        embed_kernel,
        out_shape=[shape, shape, pltpu.VMEM(routes.shape, routes.dtype), pltpu.VMEM(codes.shape, codes.dtype)],
        in_specs=[hbm()] * 5,
        out_specs=[vmem()] * 4,
        scratch_shapes=[pltpu.VMEM(tubelets.shape, BF16), pltpu.VMEM(weight.shape, BF16),
                        pltpu.VMEM((1, width), F32), pltpu.SemaphoreType.DMA((parts + 4,))],
        compiler_params=pltpu.CompilerParams(vmem_limit_bytes=VMEM_LIMIT),
        cost_estimate=pl.CostEstimate(flops=2 * tok * weight.size, bytes_accessed=weight.size * 2, transcendentals=0),
        name="embed",
    )(in_hbm(tubelets), in_hbm(weight), in_hbm(gain.reshape(1, width)), in_hbm(routes), in_hbm(codes))


def route_kernel(n_exp, half, cap, place_ref, route_ref, sib_route_ref, code_ref, sib_code_ref, select_ref, gate_ref):
    tok = code_ref.shape[1]
    both = 2 * tok
    count = n_exp * half
    slots = 2 * cap
    rows = count * slots
    routes = jnp.concatenate([route_ref[...], sib_route_ref[...]], axis=1)
    codes = jnp.concatenate([code_ref[...], sib_code_ref[...]], axis=1)
    gates = 0.25 + 0.125 * codes.astype(F32)
    plane, core = place_ref[0], place_ref[1]

    row = lax.broadcasted_iota(jnp.int32, (count, both), 0)
    expert = (plane ^ (row // half)) * (2 * half) + core * half + row % half
    first = routes[0:1] == expert
    second = routes[1:2] == expert
    member = first | second
    gated = jnp.where(first, gates[0:1, :], 0.0) + jnp.where(second, gates[1:2, :], 0.0)
    earlier = lax.broadcasted_iota(jnp.int32, (both, both), 0)
    later = lax.broadcasted_iota(jnp.int32, (both, both), 1)
    before = jnp.where(((earlier // tok) == (later // tok)) & (earlier < later), 1.0, 0.0).astype(BF16)
    rank = mm(jnp.where(member, 1.0, 0.0).astype(BF16), before)
    block = jnp.where(lax.broadcasted_iota(jnp.int32, (count, both), 1) >= tok, float(cap), 0.0)
    pos = jnp.where(member, rank + block, -1.0).astype(BF16)
    spread = jnp.where(
        lax.broadcasted_iota(jnp.int32, (rows, count), 0) // slots
        == lax.broadcasted_iota(jnp.int32, (rows, count), 1), 1.0, 0.0).astype(BF16)
    slot = (lax.broadcasted_iota(jnp.int32, (rows, both), 0) % slots).astype(F32)
    chosen = mm(spread, pos) == slot
    select_ref[...] = jnp.where(chosen, 1.0, 0.0).astype(BF16)
    gate_ref[...] = jnp.where(chosen, mm(spread, gated.astype(BF16)), 0.0).astype(BF16)


def route(place, routes, sib_routes, codes, sib_codes, n_exp, half, cap):
    both = 2 * codes.shape[1]
    rows = n_exp * half * 2 * cap
    shape = jax.ShapeDtypeStruct((rows, both), BF16)
    return pl.pallas_call(
        functools.partial(route_kernel, n_exp, half, cap),
        out_shape=[shape, shape],
        in_specs=[smem()] + [vmem()] * 4,
        out_specs=[vmem()] * 2,
        compiler_params=pltpu.CompilerParams(vmem_limit_bytes=VMEM_LIMIT),
        cost_estimate=pl.CostEstimate(flops=2 * rows * both * 64, bytes_accessed=rows * both * 4, transcendentals=0),
        name="route",
    )(place, routes, sib_routes, codes, sib_codes)


def pack_kernel(spans, select_ref, normed_ref, sib_ref, *piece_refs):
    buffer = mm(select_ref[...], jnp.concatenate([normed_ref[...], sib_ref[...]], axis=0))
    slots = piece_refs[0].shape[1]
    for (start, count), ref in zip(spans, piece_refs):
        for e in range(count):
            ref[e] = buffer[(start + e) * slots:(start + e + 1) * slots].astype(BF16)


def pack(select, normed, sib_normed, n_exp, half, cap):
    width = normed.shape[1]
    rows = select.shape[0]
    cut = early_experts(half)
    spans = []
    for s in range(n_exp):
        spans += [(s * half, half)] if s < 2 else [(s * half, cut), (s * half + cut, half - cut)]
    pieces = list(pl.pallas_call(
        functools.partial(pack_kernel, spans),
        out_shape=[pltpu.VMEM((count, 2 * cap, width), BF16) for _, count in spans],
        in_specs=[vmem()] * 3,
        out_specs=[vmem()] * len(spans),
        compiler_params=pltpu.CompilerParams(vmem_limit_bytes=VMEM_LIMIT),
        cost_estimate=pl.CostEstimate(
            flops=2 * select.size * width, bytes_accessed=rows * width * 4, transcendentals=0),
        name="pack",
    )(select, normed, sib_normed))
    return [[pieces.pop(0)] if s < 2 else [pieces.pop(0) for _ in range(CHUNKS)] for s in range(n_exp)]


def lend_kernel(place_ref, in_ref, down_ref, out_ref, sems):
    count = out_ref.shape[1]
    start = (1 - place_ref[1]) * count
    copies = []
    for e in range(count):
        for which, source in enumerate((in_ref, down_ref)):
            copies.append(pltpu.make_async_copy(source.at[start + e], out_ref.at[which, e], sems.at[which, e]))
            copies[-1].start()
    for copy in copies:
        copy.wait()


def lend(place, w_in, w_down):
    shape = (2, w_in.shape[0] // 2, *w_in.shape[1:])
    return pl.pallas_call(
        lend_kernel,
        out_shape=pltpu.VMEM(shape, BF16),
        in_specs=[smem(), hbm(), hbm()],
        out_specs=vmem(),
        scratch_shapes=[pltpu.SemaphoreType.DMA(shape[:2])],
        compiler_params=pltpu.CompilerParams(vmem_limit_bytes=VMEM_LIMIT),
        cost_estimate=pl.CostEstimate(flops=0, bytes_accessed=w_in.size * 4, transcendentals=0),
        name="lend",
    )(place, in_hbm(w_in), in_hbm(w_down))


def hold_kernel(place_ref, in_ref, down_ref, in_out, down_out, sems):
    count = in_out.shape[0]
    copies = []
    for e in range(count):
        index = place_ref[1] * count + e
        for which, (source, target) in enumerate(((in_ref, in_out), (down_ref, down_out))):
            copies.append(pltpu.make_async_copy(source.at[index], target.at[e], sems.at[which, e]))
            copies[-1].start()
    for copy in copies:
        copy.wait()


def hold(place, w_in, w_down):
    shape = pltpu.VMEM((w_in.shape[0] // 2, *w_in.shape[1:]), BF16)
    return pl.pallas_call(
        hold_kernel,
        out_shape=[shape, shape],
        in_specs=[smem(), hbm(), hbm()],
        out_specs=[vmem()] * 2,
        scratch_shapes=[pltpu.SemaphoreType.DMA((2, w_in.shape[0] // 2))],
        compiler_params=pltpu.CompilerParams(vmem_limit_bytes=VMEM_LIMIT),
        cost_estimate=pl.CostEstimate(flops=0, bytes_accessed=w_in.size * 4, transcendentals=0),
        name="hold",
    )(place, in_hbm(w_in), in_hbm(w_down))


def experts_kernel(first, *refs):
    rows_refs, (sib_ref, in_ref, down_ref), outs, h_ref = refs[:10], refs[10:13], refs[13:22], refs[22]
    far, far_a, far_b, d1, d2, own, own_a, own_b, own_d1, own_d2 = rows_refs
    per, split = far.shape[0], own_d1.shape[0]
    for e in range(per):
        mine = first + e
        own_d = own_d1[mine] if mine < split else own_d2[mine - split]
        x = jnp.concatenate(
            [ref[e] for ref in (far, far_a, far_b, d1, d2)] + [ref[mine] for ref in (own, own_a, own_b)] + [own_d], axis=0)
        h_ref[0] = jax.nn.gelu(mm(x, in_ref[mine])).astype(BF16)
        h_ref[1] = jax.nn.gelu(mm(x, sib_ref[0, mine])).astype(BF16)
        total = mm(h_ref[0], down_ref[mine], ((1,), (1,))) + mm(h_ref[1], sib_ref[1, mine], ((1,), (1,)))
        start = 0
        for ref in outs:
            ref[e] = total[start:start + ref.shape[1]].astype(BF16)
            start += ref.shape[1]


def experts(first, blocks, sib, in_own, down_own):
    far, own = blocks[0], blocks[5]
    per, far_rows, width = far.shape
    rows = 4 * (far_rows + own.shape[1])
    ff = sib.shape[3]
    shapes = [block.shape for block in blocks[:5]] + [(per, *own.shape[1:])] * 4
    return list(pl.pallas_call(
        functools.partial(experts_kernel, first),
        out_shape=[pltpu.VMEM(shape, BF16) for shape in shapes],
        in_specs=[vmem()] * 13,
        out_specs=[vmem()] * 9,
        scratch_shapes=[pltpu.VMEM((2, rows, ff), BF16)],
        compiler_params=pltpu.CompilerParams(vmem_limit_bytes=VMEM_LIMIT),
        cost_estimate=pl.CostEstimate(
            flops=2 * per * rows * width * 2 * ff * 2, bytes_accessed=per * rows * width * 4,
            transcendentals=per * rows * 2 * ff),
        name="experts",
    )(*blocks, *(in_vmem(panel) for panel in (sib, in_own, down_own))))


def combine_kernel(tok, spans, gate_ref, emb_ref, *refs):
    own_refs, (from_a_ref, from_b_ref), piece_refs = refs[:CHUNKS], refs[CHUNKS:CHUNKS + 2], refs[CHUNKS + 2:-3]
    mine_ref, send_ref, rows_ref = refs[-3:]
    slots = own_refs[0].shape[1]
    for c, ref in enumerate(own_refs):
        for e in range(ref.shape[0]):
            i = c * own_refs[0].shape[0] + e
            done = ref[e].astype(F32) + from_a_ref[i].astype(F32) + from_b_ref[i].astype(F32)
            rows_ref[i * slots:(i + 1) * slots] = done
    for start, ref in zip(spans, piece_refs):
        for e in range(ref.shape[0]):
            rows_ref[(start + e) * slots:(start + e + 1) * slots] = ref[e].astype(F32)
    total = mm(gate_ref[...], rows_ref[...].astype(BF16), ((0,), (0,)))
    mine_ref[...] = total[0:tok] + emb_ref[...].astype(F32)
    send_ref[...] = total[tok:2 * tok].astype(BF16)


def combine(gate, embedded, own_parts, from_a, from_b, spans, pieces):
    tok, width = embedded.shape
    rows = gate.shape[0]
    return pl.pallas_call(
        functools.partial(combine_kernel, tok, spans),
        out_shape=[pltpu.VMEM((tok, width), F32), pltpu.VMEM((tok, width), BF16)],
        in_specs=[vmem()] * (4 + len(own_parts) + len(pieces)),
        out_specs=[vmem()] * 2,
        scratch_shapes=[pltpu.VMEM((rows, width), F32)],
        compiler_params=pltpu.CompilerParams(vmem_limit_bytes=VMEM_LIMIT),
        cost_estimate=pl.CostEstimate(flops=4 * tok * rows * width, bytes_accessed=rows * width * 2, transcendentals=0),
        name="combine",
    )(gate, embedded, *own_parts, from_a, from_b, *pieces)


def on_device(tubelets, embed_weight, norm_gain, routes, gate_codes, w_in, w_down):
    tok = tubelets.shape[0]
    n_exp = lax.axis_size("exp")
    half = w_in.shape[0] // 2
    cap = 3 * tok // (w_in.shape[0] * n_exp)
    position = lax.axis_index("rep")
    core = position % 2
    place = jnp.stack([lax.axis_index("exp"), core]).astype(jnp.int32)

    core_bit = 1 << CORE
    routes, codes = routes.T, gate_codes.T
    sib_routes, sib_codes = swapped(routes, "rep", core_bit), swapped(codes, "rep", core_bit)
    embedded, normed, routes, codes = embed(tubelets, embed_weight, norm_gain, routes, codes)
    sib_normed = swapped(normed, "rep", core_bit)
    select, gate = route(place, routes, sib_routes, codes, sib_codes, n_exp, half, cap)

    for bit in range(GROUP_BITS, lax.axis_size("rep").bit_length() - 1):
        upper = position // (1 << bit) % 2 == 1

        def gathered(panel):
            partner = swapped(panel, "rep", 1 << bit)
            return jnp.where(upper, jnp.concatenate([partner, panel], axis=2), jnp.concatenate([panel, partner], axis=2))

        w_in, w_down = gathered(w_in), gathered(w_down)

    pieces = pack(select, normed, sib_normed, n_exp, half, cap)
    cut, split = early_experts(half), half // 2
    a_bit, b_bit = 1 << NEAR_A, 1 << NEAR_B

    def to_a(rows):
        return swapped(rows, "rep", a_bit)

    def to_b(rows):
        return swapped(rows, "rep", b_bit)

    own = pieces[0][0]
    first = swapped(pieces[1][0], "exp", 1)
    far0 = jnp.concatenate([swapped(pieces[s][0], "exp", s) for s in range(2, n_exp)] + [first[:cut]], axis=1)
    own_a, own_b = to_a(own), to_b(own)
    lent = lend(after(place, own_a), w_in, w_down)
    own_d = to_b(own_a[:split]), to_a(own_b[split:])
    far0, sib, *own_d = lax.optimization_barrier((far0, lent, *own_d))
    sib = swapped(sib, "rep", core_bit)
    shifts1 = list(range(n_exp - 1, 1, -1))
    late = lax.optimization_barrier((far0, *(pieces[s][1] for s in shifts1)))[1:]
    far1 = jnp.concatenate([first[cut:]] + [swapped(piece, "exp", s) for s, piece in zip(shifts1, late)], axis=1)
    a0, b0 = to_a(far0), to_b(far0)
    far1 = after(far1, a0, b0)
    in_own, down_own = hold(after(place, far0), w_in, w_down)
    a0, b0 = lax.optimization_barrier((a0, b0, in_own))[:2]
    turn = far0.shape[1] // 16 * 8
    d0 = to_b(a0[:, :turn]), to_a(b0[:, turn:])
    a1, b1 = to_a(far1), to_b(far1)
    parts0 = experts(0, (far0, a0, b0, *d0, own, own_a, own_b, *own_d), sib, in_own, down_own)
    a1, b1, *parts0 = lax.optimization_barrier((a1, b1, *parts0))
    r0 = to_a(parts0[3]), to_b(parts0[4])
    d1 = to_b(a1[:, :turn]), to_a(b1[:, turn:])

    def reduced(parts, r):
        return (jnp.concatenate([parts[1][:, :turn], parts[1][:, turn:] + r[1]], axis=1),
                jnp.concatenate([parts[2][:, :turn] + r[0], parts[2][:, turn:]], axis=1))

    def back(part, from_a, from_b, order):
        done = (part.astype(F32) + from_a.astype(F32) + from_b.astype(F32)).astype(BF16)
        shifts = jnp.split(done, n_exp - 1, axis=1)
        shifts = dict(zip(order, shifts))
        return shifts[1], {s: swapped(shifts[s], "exp", s) for s in order if s > 1}

    sums0 = reduced(parts0, r0)
    d1 = lax.optimization_barrier((*d1, *sums0))[:2]
    from_a0, from_b0 = to_a(sums0[0]), to_b(sums0[1])
    parts1 = experts(cut, (far1, a1, b1, *d1, own, own_a, own_b, *own_d), sib, in_own, down_own)
    parts1[3], parts1[4] = lax.optimization_barrier((parts1[3], parts1[4], from_b0))[:2]
    r1 = to_a(parts1[3]), to_b(parts1[4])
    returned0 = back(parts0[0], from_a0, from_b0, (*range(2, n_exp), 1))
    sums1 = reduced(parts1, r1)
    from_a1, from_b1 = to_a(sums1[0]), to_b(sums1[1])
    returned1 = back(parts1[0], from_a1, from_b1, (1, *shifts1))
    across = jnp.concatenate([parts0[8], parts1[8]], axis=0)
    across = after(across, from_a0, from_b0)
    own_r = to_a(across[:split]), to_b(across[split:])
    own_to_a = jnp.concatenate([parts0[6], parts1[6]], axis=0)
    own_to_b = jnp.concatenate([parts0[7], parts1[7]], axis=0)
    own_to_a = jnp.concatenate([own_to_a[:split], own_to_a[split:] + own_r[1]], axis=0)
    own_to_b = jnp.concatenate([own_to_b[:split] + own_r[0], own_to_b[split:]], axis=0)
    own_to_a, own_to_b = lax.optimization_barrier((own_to_a, own_to_b, *sums1))[:2]
    spans = [half] + [s * half + start for s in range(2, n_exp) for start in (0, cut)]
    pieces_back = [swapped(jnp.concatenate([returned0[0], returned1[0]], axis=0), "exp", 1)]
    pieces_back += [returned[s] for s in range(2, n_exp) for returned in (returned0[1], returned1[1])]
    mine, send = combine(
        gate, embedded, (parts0[5], parts1[5]), to_a(own_to_a), to_b(own_to_b), spans, pieces_back)
    other = swapped(send, "rep", 1 << CORE)
    return (mine + other.astype(F32)).astype(BF16)


def solution(mesh):
    return jax.shard_map(
        on_device,
        mesh=mesh,
        in_specs=(
            P(("rep", "exp"), None),
            P(),
            P(),
            P(("rep", "exp"), None),
            P(("rep", "exp"), None),
            P("exp", None, "rep"),
            P("exp", None, "rep"),
        ),
        out_specs=P(("rep", "exp"), None),
        check_vma=False,
    )
```
